128 devices in a mesh: rows: 8 (over y, core), cols: 16 (over x, z).
Axes of the slice: x: 4, y: 4, z: 4, core: 2. Of those that a mesh axis runs over, the one named last changes fastest.
Arguments:
- lab_factors: bfloat16 [262144, 256], P(('rows', 'cols')), may hold values from -0.75 to 0.75
- patient_factors: bfloat16 [8192, 256], P('rows'), may hold values from -1.796875 to 1.796875
- values: bfloat16 [8, 1024, 128, 128], P('rows', 'cols'), may hold values from -6 to 6
- weights: bfloat16 [8, 1024, 128, 128], P('rows', 'cols'), may hold values from 0 to 5
- tile_patient: int32 [8, 1024], P('rows', 'cols'), may hold values from 0 to 7, as said below
- tile_lab: int32 [8, 1024], P('rows', 'cols'), may hold values from 0 to 127
- tile_count: int32 [8, 16], P('rows', 'cols'), may hold values from 1 to 64, as said below
- ecg_embed: bfloat16 [8192, 256], P('rows'), may hold values from -6 to 6
- ecg_map: bfloat16 [256, 256], replicated, may hold values from -0.8984375 to 0.8984375
Outputs:
- new_patient: float32 [8192, 256], P(('rows', 'cols'))
- new_lab: float32 [16, 16384, 256], P('cols', 'rows')
The draws below stay inside these ranges and needn't reach their ends.
Inputs may be any that keep to these rules, and one draw needn't show every extreme that they name: The 64 slots of one device name distinct pairs of tile_patient and tile_lab. The slots of a device from its tile_count on are padding; some device has 64 in every draw.
All inputs are finite; a program needn't handle non-finite values.
Results may differ from the reference program's by a relative error of at most 0.0033.
Values may be sent and summed in bfloat16 or wider, within the bound.
No kernel may reach another device: no remote copies, remote signals or barrier semaphores. Data moves between devices by JAX's collectives and lax.ppermute only.
A program may use at most 128 MiB of HBM per device.

```python
import math
import jax
import jax.numpy as jnp
from jax import lax

R = 256
E = 256
TILE = 128
LT_DEV = 16
ITERS = 3
PT = 8
NT = 64
PATIENTS = 8192
LABS = 262144
CT = 128
N_ROWS = 8
N_COLS = 16


def tile_pairs(key):
    pair_key = jax.random.fold_in(key, 11)
    device_keys = jax.random.split(pair_key, N_ROWS * N_COLS)

    def one_device(device_key):
        return jax.random.permutation(device_key, PT * LT_DEV * N_ROWS)[:NT]
    chosen = jax.vmap(one_device)(device_keys)
    return chosen.reshape(N_ROWS, N_COLS * NT)


def draw_tile_patient(key, part):
    chosen = tile_pairs(key)
    return (chosen // (LT_DEV * N_ROWS)).astype(jnp.int32)


def draw_tile_lab(key, part):
    chosen = tile_pairs(key)
    return (chosen % (LT_DEV * N_ROWS)).astype(jnp.int32)


def draw_tile_count(key, part):
    key = jax.random.fold_in(key, 5)
    first_key, second_key, third_key = jax.random.split(key, 3)
    lowest = max(1, NT // 8)
    highest = NT // 2 + 1
    device_total = N_ROWS * N_COLS
    counts = jax.random.randint(first_key, (device_total,), lowest, highest)
    filled = jax.random.randint(second_key, (device_total,), 0, 8) == 0
    counts = jnp.where(filled, NT, counts)
    forced = jax.random.randint(third_key, (), 0, device_total)
    counts = counts.at[forced].set(NT)
    return counts.reshape(N_ROWS, N_COLS).astype(jnp.int32)


def draw_lab_factors(key, part):
    key = jax.random.fold_in(key, 7)
    first_key, second_key = jax.random.split(key, 2)
    column_scale = jnp.exp(jax.random.uniform(second_key, (R,), jnp.float32, math.log(0.3), math.log(3.0)))
    entries = jnp.clip(jax.random.normal(first_key, (LABS, R), jnp.float32), -4.0, 4.0)
    return (entries * column_scale / 16.0).astype(jnp.bfloat16)


def draw_weights(key, part):
    key = jax.random.fold_in(key, 9)
    first_key, second_key = jax.random.split(key)
    shape = (N_ROWS, N_COLS * NT, TILE, TILE)
    seen = jax.random.bernoulli(first_key, 0.125, shape)
    level = jnp.exp(jax.random.uniform(second_key, shape, jnp.float32, math.log(0.2), math.log(5.0)))
    return jnp.where(seen, level, 0.0).astype(jnp.bfloat16)


def level_of(own_key, shape, shards, low, top_value):
    factor_of, own = 1.0, jax.random.fold_in(own_key, 6)
    for axis_at, blocks in shards:
        steps = jnp.exp(jax.random.uniform(jax.random.fold_in(own, axis_at), (blocks,), jnp.float32, low / len(shards), top_value / len(shards)))
        factor_of = factor_of * jnp.repeat(steps, shape[axis_at] // blocks).reshape([-1 if axis == axis_at else 1 for axis in range(len(shape))])
    return factor_of


def normal_values(key, extent, scale, limit, cuts=(), held_as=jnp.bfloat16):
    values = jax.random.normal(key, extent, jnp.float32) * scale
    if len(cuts) > 0:
        values = level_of(key, extent, cuts, -0.22, 0.18) * values
    return jnp.clip(values, min=-limit, max=limit).astype(held_as)


def setup_inputs(seed: int = 0) -> dict:
    streams_of = jax.random.split(jax.random.key(seed), 10)
    return {
        "lab_factors": draw_lab_factors(jax.random.fold_in(streams_of[9], 71), 0),
        "patient_factors": normal_values(streams_of[1], (PATIENTS, R), 0.3, 1.796875, ((0, 8),)),
        "values": normal_values(streams_of[2], (N_ROWS, N_COLS * NT, TILE, TILE), 1.0, 6.0, ((0, 8), (1, 16))),
        "weights": draw_weights(jax.random.fold_in(streams_of[9], 71), 0),
        "tile_patient": draw_tile_patient(jax.random.fold_in(streams_of[9], 71), 0),
        "tile_lab": draw_tile_lab(jax.random.fold_in(streams_of[9], 71), 0),
        "tile_count": draw_tile_count(jax.random.fold_in(streams_of[9], 71), 0),
        "ecg_embed": normal_values(streams_of[7], (PATIENTS, E), 1.0, 6.0, ((0, 8),)),
        "ecg_map": normal_values(streams_of[8], (E, R), 0.15, 0.8984375),
    }


ridge_term = 1.0


def device_view(arrays, row_index, col_index):
    shaped_values, shaped_weights, patient_table, lab_table, tile_count, lab_tiles = arrays
    slot_values = shaped_values[row_index, col_index].astype(jnp.float32)
    live_mask = (jnp.arange(NT) < tile_count[row_index, col_index]).astype(jnp.float32)
    slot_weights = shaped_weights[row_index, col_index].astype(jnp.float32) * live_mask[:, None, None]
    patient_ids = patient_table[row_index, col_index]
    lab_local = lab_table[row_index, col_index]
    lab_blocks = lab_tiles[lab_local * N_COLS + col_index].astype(jnp.float32)
    return slot_values, slot_weights, patient_ids, lab_local, lab_blocks


def rounded(field_rows):
    return lax.optimization_barrier(field_rows.astype(jnp.bfloat16)).astype(jnp.float32)


def patient_partial(arrays, row_index, col_index, probe_row, with_values):
    slot_values, slot_weights, patient_ids, lab_local, lab_blocks = device_view(arrays, row_index, col_index)
    patient_blocks = probe_row[patient_ids].astype(jnp.float32)
    scores = jnp.einsum("tpr,tlr->tpl", patient_blocks, lab_blocks)
    if with_values:
        kernel = slot_weights * (slot_values - scores)
    else:
        kernel = slot_weights * scores
    contrib = jnp.einsum("tpl,tlr->tpr", rounded(kernel), lab_blocks)
    return jax.ops.segment_sum(contrib, patient_ids, num_segments=PT)


def patient_apply(arrays, probe, with_values):
    def per_row(row_index):
        def add_col(col_index, running):
            return running + patient_partial(arrays, row_index, col_index, probe[row_index], with_values)
        return lax.fori_loop(0, N_COLS, add_col, jnp.zeros((PT, TILE, R), jnp.float32))
    return lax.map(per_row, jnp.arange(N_ROWS)).reshape(PATIENTS, R)


def side_apply(field_rows, embed_map):
    inner_rows = jnp.dot(field_rows, embed_map.T, precision=lax.Precision.HIGHEST)
    return jnp.dot(inner_rows, embed_map, precision=lax.Precision.HIGHEST)


def reference(lab_factors, patient_factors, values, weights, tile_patient, tile_lab, tile_count, ecg_embed, ecg_map):
    lab_tiles = lab_factors.reshape(LABS // TILE, TILE, R)
    arrays = (values.reshape(N_ROWS, N_COLS, NT, TILE, TILE), weights.reshape(N_ROWS, N_COLS, NT, TILE, TILE),
              tile_patient.reshape(N_ROWS, N_COLS, NT), tile_lab.reshape(N_ROWS, N_COLS, NT), tile_count, lab_tiles)
    embed_map = ecg_map.astype(jnp.float32)
    solution = patient_factors.astype(jnp.float32)
    residual = patient_apply(arrays, patient_factors.reshape(N_ROWS, PT, TILE, R), True)
    residual = residual + jnp.dot(ecg_embed.astype(jnp.float32) - jnp.dot(solution, embed_map.T, precision=lax.Precision.HIGHEST), embed_map, precision=lax.Precision.HIGHEST)
    residual = residual - ridge_term * solution
    direction = residual
    norm_now = jnp.sum(residual * residual, axis=1, keepdims=True)
    for iteration in range(ITERS):
        probe = direction.astype(jnp.bfloat16).reshape(N_ROWS, PT, TILE, R)
        applied = patient_apply(arrays, probe, False) + side_apply(direction, embed_map) + ridge_term * direction
        step_size = norm_now / jnp.sum(direction * applied, axis=1, keepdims=True)
        solution = solution + step_size * direction
        residual = residual - step_size * applied
        norm_next = jnp.sum(residual * residual, axis=1, keepdims=True)
        direction = residual + (norm_next / norm_now) * direction
        norm_now = norm_next
    new_patient = solution
    factor_probe = new_patient.astype(jnp.bfloat16).reshape(N_ROWS, PT, TILE, R)

    def per_col(col_index):
        def lab_row(row_index, running):
            slot_values, slot_weights, patient_ids, lab_local, lab_blocks = device_view(arrays, row_index, col_index)
            patient_blocks = factor_probe[row_index][patient_ids].astype(jnp.float32)
            scores = jnp.einsum("tpr,tlr->tpl", patient_blocks, lab_blocks)
            kernel = rounded(slot_weights * (slot_values - scores))
            contrib = jnp.einsum("tpl,tpr->tlr", kernel, patient_blocks)
            partial_value = jax.ops.segment_sum(contrib, lab_local, num_segments=CT)
            return running + partial_value

        summed = lax.fori_loop(0, N_ROWS, lab_row, jnp.zeros((CT, TILE, R), jnp.float32))
        own_tiles = lab_tiles[jnp.arange(CT) * N_COLS + col_index].astype(jnp.float32)
        lab_residual = summed - ridge_term * own_tiles
        lab_probe = rounded(lab_residual)

        def curv_row(row_index, running):
            slot_values, slot_weights, patient_ids, lab_local, lab_blocks = device_view(arrays, row_index, col_index)
            patient_blocks = factor_probe[row_index][patient_ids].astype(jnp.float32)
            inner_scores = jnp.einsum("tpr,tlr->tpl", patient_blocks, lab_probe[lab_local])
            partial_value = jnp.sum(slot_weights * inner_scores * inner_scores, axis=1)
            return running + jax.ops.segment_sum(partial_value, lab_local, num_segments=CT)

        norm_lab = jnp.sum(lab_residual * lab_residual, axis=-1)
        curvature = lax.fori_loop(0, N_ROWS, curv_row, jnp.zeros((CT, TILE), jnp.float32)) + ridge_term * norm_lab
        updated = own_tiles + (norm_lab / curvature)[..., None] * lab_residual
        return updated.reshape(CT * TILE, R)

    new_lab = lax.map(per_col, jnp.arange(N_COLS))
    return new_patient, new_lab
```

```python
import functools

import jax
import jax.numpy as jnp
from jax import lax
from jax.experimental import pallas as pl
from jax.experimental.pallas import tpu as pltpu
from jax.sharding import PartitionSpec as P

ITERS = 3
ridge_term = 1.0
highest = lax.Precision.HIGHEST
bf16 = jnp.bfloat16
f32 = jnp.float32
MIB = 1 << 20

VMEM = pl.BlockSpec(memory_space=pltpu.VMEM)
SMEM = pl.BlockSpec(memory_space=pltpu.SMEM)
ANY = pl.BlockSpec(memory_space=pl.ANY)

GROUP = 8
PASS_TYPES = (f32, bf16, bf16, bf16)


def dot_nt(a, b):
    return lax.dot_general(a, b, (((1,), (1,)), ((), ())), preferred_element_type=f32)


def dot_nn(a, b):
    return lax.dot_general(a, b, (((1,), (0,)), ((), ())), preferred_element_type=f32)


def prep_kernel(
    tiles, slots, row_ref, patient_ref, lab_ref, count_ref, x_ref, w_ref, meta_ref, xs_ref, ws_ref, *rest
):
    pieces, tmp, order, fill = rest[:-3], rest[-3], rest[-2], rest[-1]
    n = len(pieces)
    share = x_ref.shape[2] // n
    live = count_ref[0, 0]
    row = row_ref[0]

    def clear(i, carry):
        meta_ref[0, i] = 0
        return carry

    lax.fori_loop(0, meta_ref.shape[1], clear, 0)
    for p in range(tiles + 2):
        fill[p] = 0

    def key_of(s):
        return jnp.where(s < live, patient_ref[0, s], tiles)

    def count(s, carry):
        key = key_of(s)
        fill[key + 1] = fill[key + 1] + 1
        return carry

    lax.fori_loop(0, slots, count, 0)
    for p in range(tiles + 1):
        fill[p + 1] = fill[p + 1] + fill[p]
        meta_ref[0, slots + p] = fill[p]

    def place(s, carry):
        key = key_of(s)
        at = fill[key]
        fill[key] = at + 1
        order[at] = s
        meta_ref[0, at] = lab_ref[0, s]
        return carry

    lax.fori_loop(0, slots, place, 0)

    size = x_ref.shape[1]
    eye = (
        lax.broadcasted_iota(jnp.int32, (size, size), 0)
        == lax.broadcasted_iota(jnp.int32, (size, size), 1)
    ).astype(f32).astype(bf16)

    def turn(i, carry):
        for u in range(2):
            s = i * 2 + u
            src = order[s]
            vals, wts = x_ref[src], w_ref[src]
            xs_ref[s] = vals
            ws_ref[s] = wts
            tmp[u, 0] = dot_nt(eye, vals).astype(bf16)
            tmp[u, 1] = dot_nt(eye, wts).astype(bf16)
        for u in range(2):
            s = i * 2 + u
            for k in range(n):
                at = pl.multiple_of((row ^ k) * share, share)
                pieces[k][0, s] = tmp[u, 0, pl.ds(at, share), :]
                pieces[k][1, s] = tmp[u, 1, pl.ds(at, share), :]
        return carry

    lax.fori_loop(0, slots // 2, turn, 0)


def patient_chunk(with_values, first, end, x_ref, w_ref, v_ref, patients):
    at = [jnp.maximum(jnp.minimum(first + j, end - 1), 0) for j in range(GROUP)]
    labs = jnp.concatenate([v_ref[a] for a in at], axis=0)
    wts = jnp.concatenate(
        [w_ref[at[j]].astype(f32) * (first + j < end).astype(f32) for j in range(GROUP)], axis=1
    )
    scores = dot_nt(patients, labs)
    if with_values:
        vals = jnp.concatenate([x_ref[a].astype(f32) for a in at], axis=1)
        kern = wts * (vals - scores)
    else:
        kern = wts * scores
    return dot_nn(kern.astype(bf16), labs)


def patient_sums(with_values, slots, meta_ref, x_ref, w_ref, v_ref, y_ref, out_ref, acc, arrive):
    tiles = y_ref.shape[0]
    span = 2
    for p0 in range(0, tiles, span):
        group = range(p0, p0 + span)
        bounds = [(meta_ref[0, slots + p], meta_ref[0, slots + p + 1]) for p in group]
        arrive(bounds[0][0], bounds[-1][1])
        sums = [
            patient_chunk(with_values, lo, hi, x_ref, w_ref, v_ref, y_ref[p])
            for p, (lo, hi) in zip(group, bounds)
        ]
        for j in range(span):
            acc[j] = sums[j]
        for j, (p, (lo, hi)) in enumerate(zip(group, bounds)):

            def more(i, carry, j=j, p=p, lo=lo, hi=hi):
                acc[j] += patient_chunk(
                    with_values, lo + i * GROUP, hi, x_ref, w_ref, v_ref, y_ref[p]
                )
                return carry

            lax.fori_loop(1, (hi - lo + GROUP - 1) // GROUP, more, 0)
            out_ref[p] = acc[j].astype(out_ref.dtype)


def first_pass_kernel(
    slots, meta_ref, xs_any, ws_any, lab_any, y_ref, out_ref, v_ref, x_ref, w_ref, acc, v_sem, x_sem, w_sem
):
    tiles = y_ref.shape[0]
    live = meta_ref[0, slots + tiles]
    batches = (live + GROUP - 1) // GROUP

    def v_copy(s):
        return pltpu.make_async_copy(lab_any.at[meta_ref[0, s]], v_ref.at[s], v_sem.at[s])

    def batch_copies(c):
        at = pl.ds(c * GROUP, GROUP)
        return (
            pltpu.make_async_copy(xs_any.at[at], x_ref.at[at], x_sem.at[c]),
            pltpu.make_async_copy(ws_any.at[at], w_ref.at[at], w_sem.at[c]),
        )

    def start_batch(c, carry):
        for copy in batch_copies(c):
            copy.start()

        def start_slot(s, carry):
            v_copy(s).start()
            return carry

        return lax.fori_loop(c * GROUP, jnp.minimum((c + 1) * GROUP, live), start_slot, carry)

    lax.fori_loop(0, batches, start_batch, 0)

    def wait_slot(s, carry):
        v_copy(s).wait()
        return carry

    def wait_batch(c, carry):
        for copy in batch_copies(c):
            copy.wait()
        return carry

    wait_batch(0, 0)
    wait_slot(0, 0)

    def arrive(lo, hi):
        lax.fori_loop(jnp.maximum(lo, 1), hi, wait_slot, 0)
        lax.fori_loop(
            jnp.maximum((lo + GROUP - 1) // GROUP, 1), (hi + GROUP - 1) // GROUP, wait_batch, 0
        )

    patient_sums(True, slots, meta_ref, x_ref, w_ref, v_ref, y_ref, out_ref, acc, arrive)


def pass_kernel(slots, meta_ref, w_ref, v_ref, y_ref, out_ref, acc):
    patient_sums(
        False, slots, meta_ref, None, w_ref, v_ref, y_ref, out_ref, acc, lambda lo, hi: None
    )


def spread(probe_ref, rows):
    for k in range(probe_ref.shape[0]):
        probe_ref[k] = rows


def first_kernel(recv_ref, start_ref, side_ref, gram_ref, state_ref, probe_ref):
    residual = jnp.sum(recv_ref[...].astype(f32), axis=0) + side_ref[...]
    state_ref[0] = start_ref[...].astype(f32)
    state_ref[1] = residual
    state_ref[2] = residual
    state_ref[3] = (
        jnp.dot(residual, gram_ref[...], precision=highest, preferred_element_type=f32)
        + ridge_term * residual
    )
    spread(probe_ref, residual.astype(bf16))


def step_kernel(last, recv_ref, state_in, gram_ref, state_ref, probe_ref):
    residual = state_in[1]
    direction = state_in[2]
    applied = jnp.sum(recv_ref[...].astype(f32), axis=0) + state_in[3]
    norm_now = jnp.sum(residual * residual, axis=1, keepdims=True)
    step_size = norm_now / jnp.sum(direction * applied, axis=1, keepdims=True)
    solution_now = state_in[0] + step_size * direction
    if last:
        state_ref[...] = solution_now
        spread(probe_ref, solution_now.astype(bf16))
        return
    residual = residual - step_size * applied
    norm_next = jnp.sum(residual * residual, axis=1, keepdims=True)
    direction = residual + norm_next / norm_now * direction
    state_ref[0] = solution_now
    state_ref[1] = residual
    state_ref[2] = direction
    state_ref[3] = (
        jnp.dot(direction, gram_ref[...], precision=highest, preferred_element_type=f32)
        + ridge_term * direction
    )
    spread(probe_ref, direction.astype(bf16))


def lab_kernel(slots, n, row_ref, meta_ref, *refs):
    pieces = refs[:n]
    f_own, f_two, f_six, f_top, f_low, g_own, g_two, g_six, g_top, g_low = refs[n : n + 10]
    lab_any, out_ref, xw, f_ref, v_ref, acc, probe, curv, p_sem, f_sem, v_sem = refs[n + 10 :]
    tiles = f_ref.shape[0] // n
    half = tiles // 2
    share = v_ref.shape[1]
    size = f_ref.shape[1]
    row = row_ref[0]
    v_copy = pltpu.make_async_copy(lab_any.at[:, row], v_ref, v_sem)
    v_copy.start()
    p_copies = [pltpu.make_async_copy(pieces[k], xw.at[k], p_sem.at[k]) for k in range(n)]
    whole = {0: f_own, 1: g_own, 2: f_two, 3: g_two, 6: f_six, 7: g_six}
    halves = {4: (f_top, f_low), 5: (g_top, g_low)}
    f_copies = {}
    for k, ref in whole.items():
        f_copies[k] = [
            pltpu.make_async_copy(ref, f_ref.at[pl.ds((row ^ k) * tiles, tiles)], f_sem.at[k])
        ]
    for k, pair in halves.items():
        f_copies[k] = [
            pltpu.make_async_copy(
                ref, f_ref.at[pl.ds((row ^ k) * tiles + h * half, half)], f_sem.at[n * h + k]
            )
            for h, ref in enumerate(pair)
        ]
    for k in range(n):
        p_copies[k].start()
        for copy in f_copies[k]:
            copy.start()
    acc[...] = jnp.zeros_like(acc)
    curv[...] = jnp.zeros_like(curv)
    v_copy.wait()
    for k in range(n):
        p_copies[k].wait()
        for copy in f_copies[k]:
            copy.wait()

    span = GROUP * share
    side_by_side = 4
    row_slot = lax.broadcasted_iota(jnp.int32, (span, size), 0) // share

    def take(k, source, first, end):
        base = jnp.minimum(first, slots - GROUP)
        labs = [meta_ref[source, base + j] for j in range(GROUP)]
        inside = (row_slot >= first - base) & (row_slot < end - base)
        wts = xw[k, 1, pl.ds(base, GROUP)].reshape(span, size).astype(f32)
        return base, labs, jnp.where(inside, wts, 0.0)

    def sweep(terms_of, total):
        def add(labs, terms):
            for j, t in enumerate(labs):
                total[t] += terms[j * share : (j + 1) * share]

        def of_source(k, carry):
            source = row ^ k

            def of_tiles(q, carry):
                tile = [q * side_by_side + j for j in range(side_by_side)]
                lo = [meta_ref[source, slots + p] for p in tile]
                hi = [meta_ref[source, slots + p + 1] for p in tile]
                found = [
                    terms_of(k, source, lo[j], hi[j], source * tiles + tile[j])
                    for j in range(side_by_side)
                ]
                for labs, terms in found:
                    add(labs, terms)
                for j in range(side_by_side):

                    def more(i, carry, j=j):
                        add(*terms_of(k, source, lo[j] + i * GROUP, hi[j], source * tiles + tile[j]))
                        return carry

                    lax.fori_loop(1, (hi[j] - lo[j] + GROUP - 1) // GROUP, more, 0)
                return carry

            return lax.fori_loop(0, tiles // side_by_side, of_tiles, carry)

        lax.fori_loop(0, n, of_source, 0)

    def residual_terms(k, source, first, end, at):
        base, labs, wts = take(k, source, first, end)
        rows = jnp.concatenate([v_ref[t] for t in labs], axis=0)
        vals = xw[k, 0, pl.ds(base, GROUP)].reshape(span, size).astype(f32)
        kern = (wts * (vals - dot_nt(rows, f_ref[at]))).astype(bf16)
        return labs, dot_nn(kern, f_ref[at])

    sweep(residual_terms, acc)

    block = 16

    def finish(i, carry):
        at = pl.ds(i * block, block)
        rest = acc[at] - ridge_term * v_ref[at].astype(f32)
        acc[at] = rest
        probe[at] = rest.astype(bf16)
        return carry

    lax.fori_loop(0, acc.shape[0] // block, finish, 0)

    def curvature_terms(k, source, first, end, at):
        base, labs, wts = take(k, source, first, end)
        rows = jnp.concatenate([probe[t] for t in labs], axis=0)
        inner = dot_nt(rows, f_ref[at])
        return labs, wts * inner * inner

    sweep(curvature_terms, curv)

    def emit(i, carry):
        at = pl.ds(i * block, block)
        rest = acc[at]
        norm = jnp.sum(rest * rest, axis=-1, keepdims=True)
        total = jnp.sum(curv[at], axis=-1, keepdims=True) + ridge_term * norm
        out_ref[at] = (norm / total * rest).astype(out_ref.dtype)
        return carry

    lax.fori_loop(0, acc.shape[0] // block, emit, 0)


def shape_of(shape, dtype):
    return jax.ShapeDtypeStruct(shape, dtype)


def params(mib):
    return pltpu.CompilerParams(vmem_limit_bytes=mib * MIB)


def shards(
    lab_factors,
    patient_factors,
    values,
    weights,
    tile_patient,
    tile_lab,
    tile_count,
    ecg_embed,
    ecg_map,
):
    rows = lax.axis_size("rows")
    cols = lax.axis_size("cols")
    size = values.shape[2]
    slots = values.shape[1]
    rank = lab_factors.shape[1]
    owned_tiles = lab_factors.shape[0] // size
    col_tiles = owned_tiles * rows
    patient_rows = patient_factors.shape[0]
    tiles = patient_rows // size
    share_rows = patient_rows // cols
    lab_share = size // rows
    row = lax.axis_index("rows").astype(jnp.int32).reshape(1)
    x, w = values[0], weights[0]

    own_labs = lax.all_to_all(lab_factors, "cols", split_axis=0, concat_axis=0, tiled=True)
    labs = lax.all_gather(own_labs, "rows", axis=0, tiled=True)

    slot_shape = shape_of((slots, size, size), bf16)
    out_pieces = [shape_of((2, slots, lab_share, size), bf16)] * rows
    prep = pl.pallas_call(
        functools.partial(prep_kernel, tiles, slots),
        out_shape=[shape_of((1, 128), jnp.int32), slot_shape, slot_shape] + out_pieces,
        in_specs=[SMEM] * 4 + [VMEM] * 2,
        out_specs=[SMEM] + [VMEM] * (rows + 2),
        scratch_shapes=[
            pltpu.VMEM((2, 2, size, size), bf16),
            pltpu.SMEM((slots,), jnp.int32),
            pltpu.SMEM((tiles + 2,), jnp.int32),
        ],
        compiler_params=params(28),
        name="prep",
    )(row, tile_patient, tile_lab, tile_count, x, w)
    meta, xs, ws, pieces = prep[0], prep[1], prep[2], list(prep[3:])
    meta_all = lax.all_gather(meta, "rows", axis=0, tiled=True)

    embed_map = ecg_map.astype(f32)
    gram = jnp.dot(embed_map.T, embed_map, precision=highest)
    share_at = lax.axis_index("cols") * share_rows
    start_share = lax.dynamic_slice_in_dim(patient_factors, share_at, share_rows).astype(f32)
    embed_share = lax.dynamic_slice_in_dim(ecg_embed, share_at, share_rows).astype(f32)
    side = (
        jnp.dot(
            embed_share - jnp.dot(start_share, embed_map.T, precision=highest),
            embed_map,
            precision=highest,
        )
        - ridge_term * start_share
    )

    labs, pieces, meta_all, side, gram, start_share = lax.optimization_barrier(
        (labs, pieces, meta_all, side, gram, start_share)
    )
    lab_tiles = labs.reshape(col_tiles, size, rank)

    def swap(array, k):
        return lax.ppermute(array, "rows", [(i, i ^ k) for i in range(rows)])

    def send_pieces(now, keys):
        if not keys:
            return now, lambda later: later
        held = lax.optimization_barrier((now, [pieces[k] for k in keys]))
        moved = [swap(piece, k) for piece, k in zip(held[1], keys)]

        def end(later):
            later, done = lax.optimization_barrier((later, moved))
            for k, piece in zip(keys, done):
                pieces[k] = piece
            return later

        return held[0], end

    def exchange(partial):
        partial = partial.reshape(patient_rows, rank)
        recv = lax.all_to_all(partial, "cols", split_axis=0, concat_axis=0, tiled=True)
        return recv.reshape(cols, share_rows, rank)

    def to_all(probe):
        probe = probe.reshape(patient_rows, rank)
        probe = lax.all_to_all(probe, "cols", split_axis=0, concat_axis=0, tiled=True)
        return probe.reshape(tiles, size, rank)

    state_shape = shape_of((4, share_rows, rank), f32)
    probe_shape = shape_of((cols, share_rows, rank), bf16)
    stages = ((1, 2), (3, 4), (5, 6), (7,))
    lab_tiles, end = send_pieces(lab_tiles, stages[0])
    partial, slot_labs = pl.pallas_call(
        functools.partial(first_pass_kernel, slots),
        out_shape=[
            shape_of((tiles, size, rank), PASS_TYPES[0]),
            shape_of((slots, size, rank), bf16),
        ],
        in_specs=[SMEM, ANY, ANY, ANY, VMEM],
        out_specs=[VMEM] * 2,
        scratch_shapes=[
            pltpu.VMEM((slots, size, size), bf16),
            pltpu.VMEM((slots, size, size), bf16),
            pltpu.VMEM((2, size, rank), f32),
            pltpu.SemaphoreType.DMA((slots,)),
            pltpu.SemaphoreType.DMA((slots // GROUP,)),
            pltpu.SemaphoreType.DMA((slots // GROUP,)),
        ],
        compiler_params=params(24),
        name="first_pass",
    )(meta, xs, ws, lab_tiles, patient_factors.reshape(tiles, size, rank))
    recv = end(exchange(partial))
    state, probe = pl.pallas_call(
        first_kernel,
        out_shape=[state_shape, probe_shape],
        in_specs=[VMEM] * 4,
        out_specs=[VMEM] * 2,
        compiler_params=params(8),
        name="first_step",
    )(recv, start_share, side, gram)
    for iteration in range(ITERS):
        last = iteration == ITERS - 1
        probe, end = send_pieces(probe, stages[iteration + 1])
        partial = pl.pallas_call(
            functools.partial(pass_kernel, slots),
            out_shape=shape_of((tiles, size, rank), PASS_TYPES[iteration + 1]),
            in_specs=[SMEM] + [VMEM] * 3,
            out_specs=VMEM,
            scratch_shapes=[pltpu.VMEM((2, size, rank), f32)],
            compiler_params=params(16),
            name="patient_pass",
        )(meta, ws, slot_labs, to_all(probe))
        recv = end(exchange(partial))
        state, probe = pl.pallas_call(
            functools.partial(step_kernel, last),
            out_shape=[shape_of((share_rows, rank), f32) if last else state_shape, probe_shape],
            in_specs=[VMEM] * 3,
            out_specs=[VMEM] * 2,
            compiler_params=params(8),
            name="step",
        )(recv, state, gram)
    patient_out = state

    f_own = to_all(probe)
    half = tiles // 2
    f_two, f_six = swap(f_own, 2), swap(f_own, 6)
    f_top, f_low = swap(f_six[:half], 2), swap(f_two[half:], 6)
    here = [f_own, f_two, f_six, f_top, f_low]
    factors = here + [swap(part, 1) for part in here]
    delta = pl.pallas_call(
        functools.partial(lab_kernel, slots, rows),
        out_shape=shape_of((col_tiles, lab_share, rank), bf16),
        in_specs=[SMEM] * 2 + [ANY] * (rows + len(factors) + 1),
        out_specs=VMEM,
        scratch_shapes=[
            pltpu.VMEM((rows, 2, slots, lab_share, size), bf16),
            pltpu.VMEM((rows * tiles, size, rank), bf16),
            pltpu.VMEM((col_tiles, lab_share, rank), bf16),
            pltpu.VMEM((col_tiles, lab_share, rank), f32),
            pltpu.VMEM((col_tiles, lab_share, rank), bf16),
            pltpu.VMEM((col_tiles, lab_share, size), f32),
            pltpu.SemaphoreType.DMA((rows,)),
            pltpu.SemaphoreType.DMA((2 * rows,)),
            pltpu.SemaphoreType.DMA,
        ],
        compiler_params=params(32),
        name="lab_step",
    )(row, meta_all, *pieces, *factors, lab_tiles.reshape(col_tiles, rows, lab_share, rank))
    back = lax.all_to_all(
        delta.reshape(col_tiles * lab_share, rank), "rows", split_axis=0, concat_axis=0, tiled=True
    )
    back = back.reshape(rows, owned_tiles, lab_share, rank).transpose(1, 0, 2, 3)
    updated = own_labs.reshape(owned_tiles, rows, lab_share, rank).astype(f32) + back.astype(f32)
    return (patient_out, updated.reshape(1, owned_tiles * size, rank))


def solution(mesh):
    in_specs = (
        P(("rows", "cols"), None),
        P("rows", None),
        P("rows", "cols", None, None),
        P("rows", "cols", None, None),
        P("rows", "cols"),
        P("rows", "cols"),
        P("rows", "cols"),
        P("rows", None),
        P(),
    )
    out_specs = (P(("rows", "cols"), None), P("cols", "rows", None))
    return jax.shard_map(shards, mesh=mesh, in_specs=in_specs, out_specs=out_specs, check_vma=False)
```

```python
import functools

import jax
import jax.numpy as jnp
from jax import lax
from jax.experimental import pallas as pl
from jax.experimental.pallas import tpu as pltpu
from jax.sharding import PartitionSpec as P

ITERS = 3
ridge_term = 1.0
highest = lax.Precision.HIGHEST
bf16 = jnp.bfloat16
f32 = jnp.float32
MIB = 1 << 20
BIG = 56

VMEM = pl.BlockSpec(memory_space=pltpu.VMEM)
SMEM = pl.BlockSpec(memory_space=pltpu.SMEM)
ANY = pl.BlockSpec(memory_space=pl.ANY)

GROUP = 8
SIDE = 4
PASS_TYPES = (f32, bf16)


def dot_nt(a, b):
    return lax.dot_general(a, b, (((1,), (1,)), ((), ())), preferred_element_type=f32)


def dot_nn(a, b):
    return lax.dot_general(a, b, (((1,), (0,)), ((), ())), preferred_element_type=f32)


def prep_kernel(
    tiles, slots, row_ref, patient_ref, lab_ref, count_ref, x_ref, w_ref, meta_ref, work_ref, xs_ref, ws_ref, *rest
):
    same, other, tmp, order, fill = rest[:-4], rest[-4], rest[-3], rest[-2], rest[-1]
    n = 2 * len(same)
    share = x_ref.shape[2] // n
    live = count_ref[0, 0]
    row = row_ref[0]

    def clear(i, carry):
        meta_ref[0, i] = 0
        return carry

    lax.fori_loop(0, meta_ref.shape[1], clear, 0)
    for p in range(tiles + 2):
        fill[p] = 0

    def key_of(s):
        return jnp.where(s < live, patient_ref[0, s], tiles)

    def count(s, carry):
        key = key_of(s)
        fill[key + 1] = fill[key + 1] + 1
        return carry

    lax.fori_loop(0, slots, count, 0)
    for p in range(tiles + 1):
        fill[p + 1] = fill[p + 1] + fill[p]
        meta_ref[0, slots + p] = fill[p]

    def place(s, carry):
        key = key_of(s)
        at = fill[key]
        fill[key] = at + 1
        order[at] = s
        meta_ref[0, at] = lab_ref[0, s]
        return carry

    lax.fori_loop(0, slots, place, 0)

    def no_work(i, carry):
        for f in range(4):
            work_ref[f, i] = 0
        return carry

    lax.fori_loop(0, work_ref.shape[1], no_work, 0)
    chunks = jnp.int32(0)
    for p in range(tiles):
        lo, hi = meta_ref[0, slots + p], meta_ref[0, slots + p + 1]

        def add(i, carry, p=p, lo=lo, hi=hi, chunks=chunks):
            work_ref[0, chunks + i] = p
            work_ref[1, chunks + i] = lo + i * GROUP
            work_ref[2, chunks + i] = hi
            return carry

        count_p = (hi - lo + GROUP - 1) // GROUP
        lax.fori_loop(0, count_p, add, 0)
        chunks = chunks + count_p

    def pad(i, carry):
        work_ref[2, i] = live
        work_ref[1, i] = live
        return carry

    blocks = (chunks + SIDE - 1) // SIDE
    lax.fori_loop(chunks, blocks * SIDE, pad, 0)
    work_ref[3, 0] = blocks

    size = x_ref.shape[1]
    eye = (
        lax.broadcasted_iota(jnp.int32, (size, size), 0)
        == lax.broadcasted_iota(jnp.int32, (size, size), 1)
    ).astype(f32).astype(bf16)

    def turn(i, carry):
        for u in range(2):
            s = i * 2 + u
            src = order[s]
            vals, wts = x_ref[src], w_ref[src]
            xs_ref[s] = vals
            ws_ref[s] = wts
            tmp[u, 0] = dot_nt(eye, vals).astype(bf16)
            tmp[u, 1] = dot_nt(eye, wts).astype(bf16)
        for u in range(2):
            s = i * 2 + u
            for k in range(n):
                at = pl.multiple_of((row ^ k) * share, share)
                to = same[k // 2] if k % 2 == 0 else other.at[k // 2]
                to[0, s] = tmp[u, 0, pl.ds(at, share), :]
                to[1, s] = tmp[u, 1, pl.ds(at, share), :]
        return carry

    lax.fori_loop(0, slots // 2, turn, 0)


def patient_sums(with_values, work_ref, x_ref, w_ref, v_ref, y_ref, out_ref, acc, arrive):
    acc[...] = jnp.zeros_like(acc)

    def chunk(c):
        tile, first, end = [work_ref[f, c] for f in range(3)]
        at = [jnp.maximum(jnp.minimum(first + j, end - 1), 0) for j in range(GROUP)]
        labs = jnp.concatenate([v_ref[a] for a in at], axis=0)
        wts = jnp.concatenate(
            [w_ref[a].astype(f32) * (first + j < end).astype(f32) for j, a in enumerate(at)], axis=1
        )
        scores = dot_nt(y_ref[tile], labs)
        if with_values:
            vals = jnp.concatenate([x_ref[a].astype(f32) for a in at], axis=1)
            kern = wts * (vals - scores)
        else:
            kern = wts * scores
        return tile, dot_nn(kern.astype(bf16), labs)

    def block(b, there):
        there = arrive(there, work_ref[2, b * SIDE + SIDE - 1])
        found = [chunk(b * SIDE + j) for j in range(SIDE)]
        for tile, terms in found:
            acc[tile] += terms
        return there

    lax.fori_loop(0, work_ref[3, 0], block, jnp.int32(1))
    out_ref[...] = acc[...].astype(out_ref.dtype)


def first_pass_kernel(slots, meta_ref, work_ref, *refs):
    xs_any, ws_any, lab_any, y_ref, out_ref, kept_any = refs[:6]
    v_ref, w_ref, acc, v_sem, w_sem, x_ref, x_sem, kept_sem = refs[6:]
    live = meta_ref[0, slots + y_ref.shape[0]]
    batches = (live + GROUP - 1) // GROUP

    def at(c):
        return pl.ds(c * GROUP, GROUP)

    def keep(c):
        return pltpu.make_async_copy(v_ref.at[at(c)], kept_any.at[at(c)], kept_sem.at[c])

    def rest(c, waited):
        copies = [
            pltpu.make_async_copy(ws_any.at[at(c)], w_ref.at[at(c)], w_sem.at[c]),
            pltpu.make_async_copy(xs_any.at[at(c)], x_ref.at[at(c)], x_sem.at[c]),
        ]
        if waited:
            copies.append(
                pltpu.make_async_copy(lab_any.at[pl.ds(0, GROUP)], v_ref.at[at(c)], v_sem.at[c])
            )
        return copies

    def start(c, carry):
        for j in range(GROUP):
            s = c * GROUP + j
            pltpu.make_async_copy(lab_any.at[meta_ref[0, s]], v_ref.at[s], v_sem.at[c]).start()
        for copy in rest(c, False):
            copy.start()
        return carry

    lax.fori_loop(0, batches, start, 0)

    def wait(c, carry):
        for copy in rest(c, True):
            copy.wait()
        keep(c).start()
        return carry

    wait(0, 0)

    def arrive(there, hi):
        until = jnp.maximum((hi + GROUP - 1) // GROUP, there)
        lax.fori_loop(there, until, wait, 0)
        return until

    patient_sums(True, work_ref, x_ref, w_ref, v_ref, y_ref, out_ref, acc, arrive)

    def end(c, carry):
        keep(c).wait()
        return carry

    lax.fori_loop(0, batches, end, 0)


def pass_kernel(work_ref, w_ref, v_ref, y_ref, out_ref, acc):
    patient_sums(
        False, work_ref, None, w_ref, v_ref, y_ref, out_ref, acc, lambda there, hi: there
    )


def spread(probe_ref, rows):
    for k in range(probe_ref.shape[0]):
        probe_ref[k] = rows


def first_kernel(recv_ref, start_ref, side_ref, gram_ref, state_ref, probe_ref):
    residual = jnp.sum(recv_ref[...].astype(f32), axis=0) + side_ref[...]
    state_ref[0] = start_ref[...].astype(f32)
    state_ref[1] = residual
    state_ref[2] = residual
    state_ref[3] = (
        jnp.dot(residual, gram_ref[...], precision=highest, preferred_element_type=f32)
        + ridge_term * residual
    )
    spread(probe_ref, residual.astype(bf16))


def step_kernel(turn_ref, recv_ref, state_in, gram_ref, state_ref, probe_ref):
    residual = state_in[1]
    direction = state_in[2]
    applied = jnp.sum(recv_ref[...].astype(f32), axis=0) + state_in[3]
    norm_now = jnp.sum(residual * residual, axis=1, keepdims=True)
    step_size = norm_now / jnp.sum(direction * applied, axis=1, keepdims=True)
    solution_now = state_in[0] + step_size * direction
    state_ref[0] = solution_now
    last = turn_ref[0] == ITERS - 1

    @pl.when(last)
    def _():
        spread(probe_ref, solution_now.astype(bf16))

    @pl.when(jnp.logical_not(last))
    def _():
        residual_next = residual - step_size * applied
        norm_next = jnp.sum(residual_next * residual_next, axis=1, keepdims=True)
        direction_next = residual_next + norm_next / norm_now * direction
        state_ref[1] = residual_next
        state_ref[2] = direction_next
        state_ref[3] = (
            jnp.dot(
                direction_next, gram_ref[...], precision=highest, preferred_element_type=f32
            )
            + ridge_term * direction_next
        )
        spread(probe_ref, direction_next.astype(bf16))


def lab_kernel(slots, n, row_ref, meta_ref, *refs):
    pieces, refs = refs[: n // 2], refs[n // 2 :]
    f_own, f_two, f_six, f_top, f_low, g_own, g_two, g_six, g_top, g_low = refs[:10]
    lab_any, out_ref, xw, f_ref, v_ref, acc, probe, curv, p_sem, f_sem, v_sem = refs[10:]
    tiles = f_ref.shape[0] // n
    half = tiles // 2
    share = v_ref.shape[1]
    size = f_ref.shape[1]
    row = row_ref[0]
    v_copy = pltpu.make_async_copy(lab_any.at[:, row], v_ref, v_sem)
    v_copy.start()
    factors = {0: [f_own], 1: [g_own], 2: [f_two], 3: [g_two], 6: [f_six], 7: [g_six]}
    factors |= {4: [f_top, f_low], 5: [g_top, g_low]}
    for k in range(n):
        pltpu.make_async_copy(pieces[k // 2].at[k % 2], xw.at[k], p_sem.at[k]).start()
        for h, ref in enumerate(factors[k]):
            to = pl.ds((row ^ k) * tiles + h * half, ref.shape[0])
            pltpu.make_async_copy(ref, f_ref.at[to], f_sem.at[k]).start()
    acc[...] = jnp.zeros_like(acc)
    curv[...] = jnp.zeros_like(curv)
    v_copy.wait()

    span = GROUP * share
    row_slot = lax.broadcasted_iota(jnp.int32, (span, size), 0) // share

    def sweep(terms_of, total, arrive):
        def of_source(k, carry):
            source = row ^ k
            arrive(k, source)
            lo = [meta_ref[source, slots + p] for p in range(tiles)]
            hi = [meta_ref[source, slots + p + 1] for p in range(tiles)]

            def block(i, carry):
                found = []
                for p in range(tiles):
                    first = lo[p] + i * GROUP
                    base = jnp.minimum(first, slots - GROUP)
                    labs = [meta_ref[source, base + j] for j in range(GROUP)]
                    inside = (row_slot >= first - base) & (row_slot < hi[p] - base)
                    wts = xw[k, 1, pl.ds(base, GROUP)].reshape(span, size).astype(f32)
                    wts = jnp.where(inside, wts, 0.0)
                    found.append((labs, terms_of(k, base, labs, wts, f_ref[source * tiles + p])))
                for labs, terms in found:
                    for j, t in enumerate(labs):
                        total[t] += terms[j * share : (j + 1) * share]
                return carry

            most = functools.reduce(jnp.maximum, [b - a for a, b in zip(lo, hi)])
            return lax.fori_loop(0, (most + GROUP - 1) // GROUP, block, carry)

        lax.fori_loop(0, n, of_source, 0)

    def residual_terms(k, base, labs, wts, patients):
        rows = jnp.concatenate([v_ref[t] for t in labs], axis=0)
        vals = xw[k, 0, pl.ds(base, GROUP)].reshape(span, size).astype(f32)
        return dot_nn((wts * (vals - dot_nt(rows, patients))).astype(bf16), patients)

    def arrive(k, source):
        pltpu.make_async_copy(xw.at[0], xw.at[k], p_sem.at[k]).wait()
        at = pl.ds(source * tiles, tiles)
        pltpu.make_async_copy(f_ref.at[pl.ds(0, tiles)], f_ref.at[at], f_sem.at[k]).wait()

    sweep(residual_terms, acc, arrive)

    block = 16

    def finish(i, carry):
        at = pl.ds(i * block, block)
        rest = acc[at] - ridge_term * v_ref[at].astype(f32)
        acc[at] = rest
        probe[at] = rest.astype(bf16)
        return carry

    lax.fori_loop(0, acc.shape[0] // block, finish, 0)

    def curvature_terms(k, base, labs, wts, patients):
        rows = jnp.concatenate([probe[t] for t in labs], axis=0)
        inner = dot_nt(rows, patients)
        return wts * inner * inner

    sweep(curvature_terms, curv, lambda k, source: None)

    def emit(i, carry):
        at = pl.ds(i * block, block)
        rest = acc[at]
        norm = jnp.sum(rest * rest, axis=-1, keepdims=True)
        total = jnp.sum(curv[at], axis=-1, keepdims=True) + ridge_term * norm
        out_ref[at] = (norm / total * rest).astype(out_ref.dtype)
        return carry

    lax.fori_loop(0, acc.shape[0] // block, emit, 0)


def shape_of(shape, dtype):
    return jax.ShapeDtypeStruct(shape, dtype)


def params(mib):
    return pltpu.CompilerParams(vmem_limit_bytes=mib * MIB)


def shards(
    lab_factors,
    patient_factors,
    values,
    weights,
    tile_patient,
    tile_lab,
    tile_count,
    ecg_embed,
    ecg_map,
):
    rows = lax.axis_size("rows")
    cols = lax.axis_size("cols")
    size = values.shape[2]
    slots = values.shape[1]
    rank = lab_factors.shape[1]
    owned_tiles = lab_factors.shape[0] // size
    col_tiles = owned_tiles * rows
    patient_rows = patient_factors.shape[0]
    tiles = patient_rows // size
    share_rows = patient_rows // cols
    lab_share = size // rows
    row = lax.axis_index("rows").astype(jnp.int32).reshape(1)
    x, w = values[0], weights[0]

    own_labs = lax.all_to_all(lab_factors, "cols", split_axis=0, concat_axis=0, tiled=True)
    labs = lax.all_gather(own_labs, "rows", axis=0, tiled=True)

    slot_shape = shape_of((slots, size, size), bf16)
    piece = (2, slots, lab_share, size)
    out_pieces = [shape_of(piece, bf16)] * (rows // 2) + [shape_of((rows // 2, *piece), bf16)]
    prep = pl.pallas_call(
        functools.partial(prep_kernel, tiles, slots),
        out_shape=[shape_of((1, 128), jnp.int32), shape_of((4, 128), jnp.int32)]
        + [slot_shape] * 2
        + out_pieces,
        in_specs=[SMEM] * 4 + [VMEM] * 2,
        out_specs=[SMEM] * 2 + [VMEM] * (2 + len(out_pieces)),
        scratch_shapes=[
            pltpu.VMEM((2, 2, size, size), bf16),
            pltpu.SMEM((slots,), jnp.int32),
            pltpu.SMEM((tiles + 2,), jnp.int32),
        ],
        compiler_params=params(BIG),
        name="prep",
    )(row, tile_patient, tile_lab, tile_count, x, w)
    (meta, work, xs, ws), same, other = prep[:4], prep[4:-1], prep[-1]

    def swap(array, k):
        return lax.ppermute(array, "rows", [(i, i ^ k) for i in range(rows)])

    other = swap(other, 1)
    pieces = [jnp.stack([same[h], other[h]]) for h in range(rows // 2)]
    meta_all = lax.all_gather(meta, "rows", axis=0, tiled=True)

    embed_map = ecg_map.astype(f32)
    gram = jnp.dot(embed_map.T, embed_map, precision=highest)
    share_at = lax.axis_index("cols") * share_rows
    start_share = lax.dynamic_slice_in_dim(patient_factors, share_at, share_rows).astype(f32)
    embed_share = lax.dynamic_slice_in_dim(ecg_embed, share_at, share_rows).astype(f32)
    side = (
        jnp.dot(
            embed_share - jnp.dot(start_share, embed_map.T, precision=highest),
            embed_map,
            precision=highest,
        )
        - ridge_term * start_share
    )

    labs, pieces, meta_all, side, gram, start_share = lax.optimization_barrier(
        (labs, pieces, meta_all, side, gram, start_share)
    )
    lab_tiles = labs.reshape(col_tiles, size, rank)

    pieces = [pieces[0]] + [swap(pieces[h], 2 * h) for h in range(1, rows // 2)]

    def exchange(partial):
        partial = partial.reshape(patient_rows, rank)
        recv = lax.all_to_all(partial, "cols", split_axis=0, concat_axis=0, tiled=True)
        return recv.reshape(cols, share_rows, rank)

    def to_all(probe):
        probe = probe.reshape(patient_rows, rank)
        probe = lax.all_to_all(probe, "cols", split_axis=0, concat_axis=0, tiled=True)
        return probe.reshape(tiles, size, rank)

    state_shape = shape_of((4, share_rows, rank), f32)
    probe_shape = shape_of((cols, share_rows, rank), bf16)
    batches = slots // GROUP
    partial, slot_labs = pl.pallas_call(
        functools.partial(first_pass_kernel, slots),
        out_shape=[
            shape_of((tiles, size, rank), PASS_TYPES[0]),
            shape_of((slots, size, rank), bf16),
        ],
        in_specs=[SMEM] * 2 + [ANY] * 3 + [VMEM],
        out_specs=[VMEM, ANY],
        scratch_shapes=[
            pltpu.VMEM((slots, size, rank), bf16),
            pltpu.VMEM((slots, size, size), bf16),
            pltpu.VMEM((tiles, size, rank), f32),
            pltpu.SemaphoreType.DMA((batches,)),
            pltpu.SemaphoreType.DMA((batches,)),
            pltpu.VMEM((slots, size, size), bf16),
            pltpu.SemaphoreType.DMA((batches,)),
            pltpu.SemaphoreType.DMA((batches,)),
        ],
        compiler_params=params(BIG),
        name="first_pass",
    )(meta, work, xs, ws, lab_tiles, patient_factors.reshape(tiles, size, rank))
    state, probe = pl.pallas_call(
        first_kernel,
        out_shape=[state_shape, probe_shape],
        in_specs=[VMEM] * 4,
        out_specs=[VMEM] * 2,
        compiler_params=params(8),
        name="first_step",
    )(exchange(partial), start_share, side, gram)

    def turn(iteration, carry):
        state, probe = carry
        partial = pl.pallas_call(
            pass_kernel,
            out_shape=shape_of((tiles, size, rank), PASS_TYPES[1]),
            in_specs=[SMEM] + [VMEM] * 3,
            out_specs=VMEM,
            scratch_shapes=[pltpu.VMEM((tiles, size, rank), f32)],
            compiler_params=params(16),
            name="patient_pass",
        )(work, ws, slot_labs, to_all(probe))
        state, probe = pl.pallas_call(
            step_kernel,
            out_shape=[state_shape, probe_shape],
            in_specs=[SMEM] + [VMEM] * 3,
            out_specs=[VMEM] * 2,
            compiler_params=params(8),
            name="step",
        )(iteration.reshape(1), exchange(partial), state, gram)
        return state, probe

    state, probe = lax.fori_loop(0, ITERS, turn, (state, probe))
    patient_out = state[0]

    f_own = to_all(probe)
    half = tiles // 2
    f_two, f_six = swap(f_own, 2), swap(f_own, 6)
    f_top, f_low = swap(f_six[:half], 2), swap(f_two[half:], 6)
    here = [f_own, f_two, f_six, f_top, f_low]
    factors = here + [swap(part, 1) for part in here]
    delta = pl.pallas_call(
        functools.partial(lab_kernel, slots, rows),
        out_shape=shape_of((col_tiles, lab_share, rank), bf16),
        in_specs=[SMEM] * 2 + [ANY] * (len(pieces) + len(factors) + 1),
        out_specs=VMEM,
        scratch_shapes=[
            pltpu.VMEM((rows, 2, slots, lab_share, size), bf16),
            pltpu.VMEM((rows * tiles, size, rank), bf16),
            pltpu.VMEM((col_tiles, lab_share, rank), bf16),
            pltpu.VMEM((col_tiles, lab_share, rank), f32),
            pltpu.VMEM((col_tiles, lab_share, rank), bf16),
            pltpu.VMEM((col_tiles, lab_share, size), f32),
            pltpu.SemaphoreType.DMA((rows,)),
            pltpu.SemaphoreType.DMA((rows,)),
            pltpu.SemaphoreType.DMA,
        ],
        compiler_params=params(BIG),
        name="lab_step",
    )(row, meta_all, *pieces, *factors, lab_tiles.reshape(col_tiles, rows, lab_share, rank))
    back = lax.all_to_all(
        delta.reshape(col_tiles * lab_share, rank), "rows", split_axis=0, concat_axis=0, tiled=True
    )
    back = back.reshape(rows, owned_tiles, lab_share, rank).transpose(1, 0, 2, 3)
    updated = own_labs.reshape(owned_tiles, rows, lab_share, rank).astype(f32) + back.astype(f32)
    return (patient_out, updated.reshape(1, owned_tiles * size, rank))


def solution(mesh):
    in_specs = (
        P(("rows", "cols"), None),
        P("rows", None),
        P("rows", "cols", None, None),
        P("rows", "cols", None, None),
        P("rows", "cols"),
        P("rows", "cols"),
        P("rows", "cols"),
        P("rows", None),
        P(),
    )
    out_specs = (P(("rows", "cols"), None), P("cols", "rows", None))
    return jax.shard_map(shards, mesh=mesh, in_specs=in_specs, out_specs=out_specs, check_vma=False)
```

```python
import functools

import jax
import jax.numpy as jnp
from jax import lax
from jax.experimental import pallas as pl
from jax.experimental.pallas import tpu as pltpu
from jax.sharding import PartitionSpec as P

ITERS = 3
ridge_term = 1.0
highest = lax.Precision.HIGHEST
bf16 = jnp.bfloat16
f32 = jnp.float32
MIB = 1 << 20
BIG = 56

VMEM = pl.BlockSpec(memory_space=pltpu.VMEM)
SMEM = pl.BlockSpec(memory_space=pltpu.SMEM)
ANY = pl.BlockSpec(memory_space=pl.ANY)

GROUP = 8
CHUNK = 6
LAB_CHUNK = 8
TURNS = 4
SIDE = 4
PASS_TYPES = (f32, bf16)


def dot_nt(a, b):
    return lax.dot_general(a, b, (((1,), (1,)), ((), ())), preferred_element_type=f32)


def dot_nn(a, b):
    return lax.dot_general(a, b, (((1,), (0,)), ((), ())), preferred_element_type=f32)


def prep_kernel(
    tiles, slots, row_ref, patient_ref, lab_ref, count_ref, x_ref, w_ref, meta_ref, work_ref, xs_ref, ws_ref, *rest
):
    same, other, tmp, order, fill = rest[:-4], rest[-4], rest[-3], rest[-2], rest[-1]
    n = 2 * len(same)
    pieces = [same[k // 2] if k % 2 == 0 else other.at[k // 2] for k in range(n)]
    share = x_ref.shape[2] // n
    live = count_ref[0, 0]
    row = row_ref[0]

    def clear(i, carry):
        meta_ref[0, i] = 0
        return carry

    lax.fori_loop(0, meta_ref.shape[1], clear, 0)
    for p in range(tiles + 2):
        fill[p] = 0

    def key_of(s):
        return jnp.where(s < live, patient_ref[0, s], tiles)

    def count(s, carry):
        key = key_of(s)
        fill[key + 1] = fill[key + 1] + 1
        return carry

    lax.fori_loop(0, slots, count, 0)
    for p in range(tiles + 1):
        fill[p + 1] = fill[p + 1] + fill[p]
        meta_ref[0, slots + p] = fill[p]

    def place(s, carry):
        key = key_of(s)
        at = fill[key]
        fill[key] = at + 1
        order[at] = s
        meta_ref[0, at] = lab_ref[0, s]
        return carry

    lax.fori_loop(0, slots, place, 0)

    def no_work(i, carry):
        for f in range(4):
            work_ref[f, i] = 0
        return carry

    lax.fori_loop(0, work_ref.shape[1], no_work, 0)
    chunks = jnp.int32(0)
    for p in range(tiles):
        lo, hi = meta_ref[0, slots + p], meta_ref[0, slots + p + 1]

        def add(i, carry, p=p, lo=lo, hi=hi, chunks=chunks):
            work_ref[0, chunks + i] = p
            work_ref[1, chunks + i] = lo + i * CHUNK
            work_ref[2, chunks + i] = hi
            return carry

        count_p = (hi - lo + CHUNK - 1) // CHUNK
        lax.fori_loop(0, count_p, add, 0)
        chunks = chunks + count_p

    def pad(i, carry):
        work_ref[2, i] = live
        work_ref[1, i] = live
        return carry

    blocks = (chunks + SIDE - 1) // SIDE
    lax.fori_loop(chunks, blocks * SIDE, pad, 0)
    work_ref[3, 0] = blocks

    lane = lax.broadcasted_iota(jnp.int32, (share, meta_ref.shape[1]), 1)
    table = jnp.zeros(lane.shape, f32)
    for i in range(slots + tiles + 1):
        table = jnp.where(lane == i, meta_ref[0, i].astype(f32), table)
    for k in range(n):
        pieces[k][2 * slots] = table.astype(bf16)

    size = x_ref.shape[1]
    eye = (
        lax.broadcasted_iota(jnp.int32, (size, size), 0)
        == lax.broadcasted_iota(jnp.int32, (size, size), 1)
    ).astype(f32).astype(bf16)

    def turn(i, carry):
        for u in range(TURNS):
            s = i * TURNS + u
            src = order[s]
            vals, wts = x_ref[src], w_ref[src]
            xs_ref[s] = vals
            ws_ref[s] = wts
            tmp[u, 0] = dot_nt(eye, vals).astype(bf16)
            tmp[u, 1] = dot_nt(eye, wts).astype(bf16)
        for u in range(TURNS):
            s = i * TURNS + u
            for k in range(n):
                at = pl.multiple_of((row ^ k) * share, share)
                pieces[k][s] = tmp[u, 0, pl.ds(at, share), :]
                pieces[k][slots + s] = tmp[u, 1, pl.ds(at, share), :]
        return carry

    lax.fori_loop(0, slots // TURNS, turn, 0)


def patient_sums(
    with_values, work_ref, x_ref, w_ref, labs_of, y_ref, out_ref, acc, arrive
):
    acc[...] = jnp.zeros_like(acc)

    def chunk(c):
        tile, first, end = [work_ref[f, c] for f in range(3)]
        at = [jnp.maximum(jnp.minimum(first + j, end - 1), 0) for j in range(CHUNK)]
        labs = jnp.concatenate([labs_of(a) for a in at], axis=0)
        wts = jnp.concatenate(
            [w_ref[a].astype(f32) * (first + j < end).astype(f32) for j, a in enumerate(at)], axis=1
        )
        scores = dot_nt(y_ref[tile], labs)
        if with_values:
            vals = jnp.concatenate([x_ref[a].astype(f32) for a in at], axis=1)
            kern = wts * (vals - scores)
        else:
            kern = wts * scores
        return tile, dot_nn(kern.astype(bf16), labs)

    def block(b, there):
        there = arrive(there, work_ref[2, b * SIDE + SIDE - 1])
        found = [chunk(b * SIDE + j) for j in range(SIDE)]
        for tile, terms in found:
            acc[tile] += terms
        return there

    lax.fori_loop(0, work_ref[3, 0], block, jnp.int32(1))
    out_ref[...] = acc[...].astype(out_ref.dtype)


def first_pass_kernel(
    slots, n, row_ref, meta_ref, work_ref, xs_any, ws_any, y_ref, early_any, here_any, there_any, *refs
):
    out_ref, kept_any, v_ref, w_ref, x_ref, acc, v_sem, w_sem, x_sem, kept_sem = refs
    row = row_ref[0]
    live = meta_ref[0, slots + y_ref.shape[0]]
    batches = (live + GROUP - 1) // GROUP
    owned = early_any.shape[0] // n
    early = early_any.shape[1]
    late = v_ref.shape[1] - early

    def at(c):
        return pl.ds(c * GROUP, GROUP)

    def rest(c):
        return (
            pltpu.make_async_copy(ws_any.at[at(c)], w_ref.at[at(c)], w_sem.at[c]),
            pltpu.make_async_copy(xs_any.at[at(c)], x_ref.at[at(c)], x_sem.at[c]),
        )

    def keep(c):
        return pltpu.make_async_copy(v_ref.at[at(c)], kept_any.at[at(c)], kept_sem.at[c])

    def start(c, carry):
        for j in range(GROUP):
            s = c * GROUP + j
            tile = meta_ref[0, s]
            source = row ^ (tile // owned)
            pltpu.make_async_copy(
                early_any.at[tile], v_ref.at[s, pl.ds(0, early), :], v_sem.at[c]
            ).start()
            for core, late_any in enumerate((here_any, there_any)):

                @pl.when(source % 2 == core)
                def _(late_any=late_any, s=s, tile=tile, source=source):
                    pltpu.make_async_copy(
                        late_any.at[tile % owned, source // 2],
                        v_ref.at[s, pl.ds(early, late), :],
                        v_sem.at[c],
                    ).start()

        for copy in rest(c):
            copy.start()
        return carry

    lax.fori_loop(0, batches, start, 0)

    def wait(c, carry):
        for copy in rest(c):
            copy.wait()
        pltpu.make_async_copy(kept_any.at[at(c)], v_ref.at[at(c)], v_sem.at[c]).wait()
        keep(c).start()
        return carry

    wait(0, 0)

    def arrive(there, hi):
        until = jnp.maximum((hi + GROUP - 1) // GROUP, there)
        lax.fori_loop(there, until, wait, 0)
        return until

    patient_sums(
        True, work_ref, x_ref, w_ref, lambda s: v_ref[s], y_ref, out_ref, acc, arrive
    )

    def end(c, carry):
        keep(c).wait()
        return carry

    lax.fori_loop(0, batches, end, 0)


def pass_kernel(slots, meta_ref, work_ref, w_ref, kept_any, y_ref, out_ref, v_ref, acc, v_sem):
    batches = (meta_ref[0, slots + y_ref.shape[0]] + GROUP - 1) // GROUP

    def copy(c):
        at = pl.ds(c * GROUP, GROUP)
        return pltpu.make_async_copy(kept_any.at[at], v_ref.at[at], v_sem.at[c])

    def start(c, carry):
        copy(c).start()
        return carry

    def wait(c, carry):
        copy(c).wait()
        return carry

    lax.fori_loop(0, batches, start, 0)
    wait(0, 0)

    def arrive(there, hi):
        until = jnp.maximum((hi + GROUP - 1) // GROUP, there)
        lax.fori_loop(there, until, wait, 0)
        return until

    patient_sums(
        False, work_ref, None, w_ref, lambda s: v_ref[s], y_ref, out_ref, acc, arrive
    )


def spread(probe_ref, rows):
    for k in range(probe_ref.shape[0]):
        probe_ref[k] = rows


def first_kernel(recv_ref, start_ref, side_ref, gram_ref, state_ref, probe_ref):
    residual = jnp.sum(recv_ref[...].astype(f32), axis=0) + side_ref[...]
    state_ref[0] = start_ref[...].astype(f32)
    state_ref[1] = residual
    state_ref[2] = residual
    state_ref[3] = (
        jnp.dot(residual, gram_ref[...], precision=highest, preferred_element_type=f32)
        + ridge_term * residual
    )
    spread(probe_ref, residual.astype(bf16))


def step_kernel(turn_ref, recv_ref, state_in, gram_ref, state_ref, probe_ref):
    residual = state_in[1]
    direction = state_in[2]
    applied = jnp.sum(recv_ref[...].astype(f32), axis=0) + state_in[3]
    norm_now = jnp.sum(residual * residual, axis=1, keepdims=True)
    step_size = norm_now / jnp.sum(direction * applied, axis=1, keepdims=True)
    solution_now = state_in[0] + step_size * direction
    state_ref[0] = solution_now
    last = turn_ref[0] == ITERS - 1

    @pl.when(last)
    def _():
        spread(probe_ref, solution_now.astype(bf16))

    @pl.when(jnp.logical_not(last))
    def _():
        residual_next = residual - step_size * applied
        norm_next = jnp.sum(residual_next * residual_next, axis=1, keepdims=True)
        direction_next = residual_next + norm_next / norm_now * direction
        state_ref[1] = residual_next
        state_ref[2] = direction_next
        state_ref[3] = (
            jnp.dot(
                direction_next, gram_ref[...], precision=highest, preferred_element_type=f32
            )
            + ridge_term * direction_next
        )
        spread(probe_ref, direction_next.astype(bf16))


def lab_kernel(slots, n, row_ref, same_any, other_any, *refs):
    pieces = [same_any, other_any.at[0]]
    for ref in refs[: n // 2 - 1]:
        pieces += [ref.at[0], ref.at[1]]
    refs = refs[n // 2 - 1 :]
    f_own, f_two, f_six, f_top, f_low, g_own, g_two, g_six, g_top, g_low = refs[:10]
    early_any, here_any, there_any, out_ref, xw, f_ref, v_ref, acc, probe, curv, p_sem, f_sem, v_sem = refs[10:23]
    coded, table, meta_ref, t_sem, m_sem = refs[23:]
    tiles = f_ref.shape[0] // n
    half = tiles // 2
    share = v_ref.shape[1]
    size = f_ref.shape[1]
    row = row_ref[0]
    t_copies = [
        pltpu.make_async_copy(pieces[k].at[2 * slots], coded.at[k], t_sem.at[k]) for k in range(n)
    ]
    for copy in t_copies:
        copy.start()
    early = early_any.shape[1] // share
    owned = v_ref.shape[0] // n

    @pl.when(row < early)
    def _():
        at = pl.ds(row * share, share)
        pltpu.make_async_copy(early_any.at[:, at, :], v_ref, v_sem).start()

    @pl.when(row >= early)
    def _():
        at = pl.ds((row - early) * share, share)
        for k in range(n):
            part = (here_any, there_any)[k % 2].at[:, k // 2, at, :]
            to = pl.ds((row ^ k) * owned, owned)
            pltpu.make_async_copy(part, v_ref.at[to], v_sem).start()

    factors = {0: [f_own], 1: [g_own], 2: [f_two], 3: [g_two], 6: [f_six], 7: [g_six]}
    factors |= {4: [f_top, f_low], 5: [g_top, g_low]}
    for k in range(n):
        pltpu.make_async_copy(pieces[k], xw.at[k], p_sem.at[k]).start()
        for h, ref in enumerate(factors[k]):
            to = pl.ds((row ^ k) * tiles + h * half, ref.shape[0])
            pltpu.make_async_copy(ref, f_ref.at[to], f_sem.at[k]).start()
    for k, copy in enumerate(t_copies):
        copy.wait()
        table[k : k + 1] = coded[k, 0:1].astype(f32).astype(jnp.int32)
    m_copy = pltpu.make_async_copy(table, meta_ref, m_sem)
    m_copy.start()
    acc[...] = jnp.zeros_like(acc)
    curv[...] = jnp.zeros_like(curv)
    m_copy.wait()
    pltpu.make_async_copy(v_ref, v_ref, v_sem).wait()

    span = LAB_CHUNK * share
    row_slot = lax.broadcasted_iota(jnp.int32, (span, size), 0) // share

    def sweep(terms_of, total, arrive):
        def of_source(k, carry):
            source = row ^ k
            arrive(k, source)
            lo = [meta_ref[k, slots + p] for p in range(tiles)]
            hi = [meta_ref[k, slots + p + 1] for p in range(tiles)]

            def block(i, carry):
                found = []
                for p in range(tiles):
                    first = lo[p] + i * LAB_CHUNK
                    base = jnp.minimum(first, slots - LAB_CHUNK)
                    labs = [meta_ref[k, base + j] for j in range(LAB_CHUNK)]
                    inside = (row_slot >= first - base) & (row_slot < hi[p] - base)
                    wts = xw[k, pl.ds(slots + base, LAB_CHUNK)].reshape(span, size).astype(f32)
                    wts = jnp.where(inside, wts, 0.0)
                    found.append((labs, terms_of(k, base, labs, wts, f_ref[source * tiles + p])))
                for labs, terms in found:
                    for j, t in enumerate(labs):
                        total[t] += terms[j * share : (j + 1) * share]
                return carry

            most = functools.reduce(jnp.maximum, [b - a for a, b in zip(lo, hi)])
            return lax.fori_loop(0, (most + LAB_CHUNK - 1) // LAB_CHUNK, block, carry)

        lax.fori_loop(0, n, of_source, 0)

    def residual_terms(k, base, labs, wts, patients):
        rows = jnp.concatenate([v_ref[t] for t in labs], axis=0)
        vals = xw[k, pl.ds(base, LAB_CHUNK)].reshape(span, size).astype(f32)
        return dot_nn((wts * (vals - dot_nt(rows, patients))).astype(bf16), patients)

    def arrive(k, source):
        pltpu.make_async_copy(xw.at[0], xw.at[k], p_sem.at[k]).wait()
        at = pl.ds(source * tiles, tiles)
        pltpu.make_async_copy(f_ref.at[pl.ds(0, tiles)], f_ref.at[at], f_sem.at[k]).wait()

    sweep(residual_terms, acc, arrive)

    block = 16

    def finish(i, carry):
        at = pl.ds(i * block, block)
        rest = acc[at] - ridge_term * v_ref[at].astype(f32)
        acc[at] = rest
        probe[at] = rest.astype(bf16)
        return carry

    lax.fori_loop(0, acc.shape[0] // block, finish, 0)

    def curvature_terms(k, base, labs, wts, patients):
        rows = jnp.concatenate([probe[t] for t in labs], axis=0)
        inner = dot_nt(rows, patients)
        return wts * inner * inner

    sweep(curvature_terms, curv, lambda k, source: None)

    def emit(i, carry):
        at = pl.ds(i * block, block)
        rest = acc[at]
        norm = jnp.sum(rest * rest, axis=-1, keepdims=True)
        total = jnp.sum(curv[at], axis=-1, keepdims=True) + ridge_term * norm
        out_ref[at] = (norm / total * rest).astype(out_ref.dtype)
        return carry

    lax.fori_loop(0, acc.shape[0] // block, emit, 0)


def shape_of(shape, dtype):
    return jax.ShapeDtypeStruct(shape, dtype)


def params(mib):
    return pltpu.CompilerParams(vmem_limit_bytes=mib * MIB)


def shards(
    lab_factors,
    patient_factors,
    values,
    weights,
    tile_patient,
    tile_lab,
    tile_count,
    ecg_embed,
    ecg_map,
):
    rows = lax.axis_size("rows")
    cols = lax.axis_size("cols")
    size = values.shape[2]
    slots = values.shape[1]
    rank = lab_factors.shape[1]
    owned_tiles = lab_factors.shape[0] // size
    col_tiles = owned_tiles * rows
    patient_rows = patient_factors.shape[0]
    tiles = patient_rows // size
    share_rows = patient_rows // cols
    lab_share = size // rows
    row = lax.axis_index("rows").astype(jnp.int32).reshape(1)
    x, w = values[0], weights[0]

    def swap(array, k):
        return lax.ppermute(array, "rows", [(i, i ^ k) for i in range(rows)])

    def to_columns(array):
        return lax.all_to_all(array, "cols", split_axis=0, concat_axis=0, tiled=True)

    slot_shape = shape_of((slots, size, size), bf16)
    piece = (2 * slots + 1, lab_share, size)
    out_pieces = [shape_of(piece, bf16)] * (rows // 2) + [shape_of((rows // 2, *piece), bf16)]
    prep = pl.pallas_call(
        functools.partial(prep_kernel, tiles, slots),
        out_shape=[shape_of((1, 128), jnp.int32), shape_of((4, 128), jnp.int32)]
        + [slot_shape] * 2
        + out_pieces,
        in_specs=[SMEM] * 4 + [VMEM] * 2,
        out_specs=[SMEM] * 2 + [VMEM] * (2 + len(out_pieces)),
        scratch_shapes=[
            pltpu.VMEM((TURNS, 2, size, size), bf16),
            pltpu.SMEM((slots,), jnp.int32),
            pltpu.SMEM((tiles + 2,), jnp.int32),
        ],
        compiler_params=params(BIG),
        cost_estimate=pl.CostEstimate(flops=10**9, bytes_accessed=48 * MIB, transcendentals=0),
        name="prep",
    )(row, tile_patient, tile_lab, tile_count, x, w)
    (meta, work, xs, ws), same, other = prep[:4], prep[4:-1], prep[-1]

    early = size - size // 4
    given = lab_factors.reshape(owned_tiles, size, rank)
    late = given[:, early:]
    late = [late] + [swap(late, 2 * h) for h in range(1, rows // 2)]
    own = to_columns(given[:, :early])
    labs = lax.all_gather(own, "rows", axis=0, tiled=True)
    late, _ = lax.optimization_barrier((late, own))
    late_here = to_columns(jnp.stack(late, axis=1))
    late_there = swap(late_here, 1)
    other = swap(other, 1)

    embed_map = ecg_map.astype(f32)
    gram = jnp.dot(embed_map.T, embed_map, precision=highest)
    share_at = lax.axis_index("cols") * share_rows
    start_share = lax.dynamic_slice_in_dim(patient_factors, share_at, share_rows).astype(f32)
    embed_share = lax.dynamic_slice_in_dim(ecg_embed, share_at, share_rows).astype(f32)
    side = (
        jnp.dot(
            embed_share - jnp.dot(start_share, embed_map.T, precision=highest),
            embed_map,
            precision=highest,
        )
        - ridge_term * start_share
    )

    labs, late_here, late_there, same, other = lax.optimization_barrier(
        (labs, late_here, late_there, same, other)
    )
    pieces = [jnp.stack([same[h], other[h]]) for h in range(1, rows // 2)]
    pieces = [swap(piece, 2 * h) for h, piece in enumerate(pieces, 1)]

    def exchange(partial):
        partial = partial.reshape(patient_rows, rank)
        recv = lax.all_to_all(partial, "cols", split_axis=0, concat_axis=0, tiled=True)
        return recv.reshape(cols, share_rows, rank)

    def to_all(probe):
        probe = probe.reshape(patient_rows, rank)
        probe = lax.all_to_all(probe, "cols", split_axis=0, concat_axis=0, tiled=True)
        return probe.reshape(tiles, size, rank)

    state_shape = shape_of((4, share_rows, rank), f32)
    probe_shape = shape_of((cols, share_rows, rank), bf16)
    batches = slots // GROUP
    partial, slot_labs = pl.pallas_call(
        functools.partial(first_pass_kernel, slots, rows),
        out_shape=[
            shape_of((tiles, size, rank), PASS_TYPES[0]),
            shape_of((slots, size, rank), bf16),
        ],
        in_specs=[SMEM] * 3 + [ANY] * 2 + [VMEM] + [ANY] * 3,
        out_specs=[VMEM, ANY],
        scratch_shapes=[
            pltpu.VMEM((slots, size, rank), bf16),
            pltpu.VMEM((slots, size, size), bf16),
            pltpu.VMEM((slots, size, size), bf16),
            pltpu.VMEM((tiles, size, rank), f32),
        ]
        + [pltpu.SemaphoreType.DMA((batches,))] * 4,
        compiler_params=params(BIG),
        name="first_pass",
    )(
        row,
        meta,
        work,
        xs,
        ws,
        patient_factors.reshape(tiles, size, rank),
        labs,
        late_here,
        late_there,
    )
    state, probe = pl.pallas_call(
        first_kernel,
        out_shape=[state_shape, probe_shape],
        in_specs=[VMEM] * 4,
        out_specs=[VMEM] * 2,
        compiler_params=params(8),
        name="first_step",
    )(exchange(partial), start_share, side, gram)

    def turn(iteration, carry):
        state, probe = carry
        partial = pl.pallas_call(
            functools.partial(pass_kernel, slots),
            out_shape=shape_of((tiles, size, rank), PASS_TYPES[1]),
            in_specs=[SMEM] * 2 + [VMEM, ANY, VMEM],
            out_specs=VMEM,
            scratch_shapes=[
                pltpu.VMEM((slots, size, rank), bf16),
                pltpu.VMEM((tiles, size, rank), f32),
                pltpu.SemaphoreType.DMA((batches,)),
            ],
            compiler_params=params(24),
            name="patient_pass",
        )(meta, work, ws, slot_labs, to_all(probe))
        state, probe = pl.pallas_call(
            step_kernel,
            out_shape=[state_shape, probe_shape],
            in_specs=[SMEM] + [VMEM] * 3,
            out_specs=[VMEM] * 2,
            compiler_params=params(8),
            name="step",
        )(iteration.reshape(1), exchange(partial), state, gram)
        return state, probe

    state, probe = lax.fori_loop(0, ITERS, turn, (state, probe))
    patient_out = state[0]

    f_own = to_all(probe)
    half = tiles // 2
    f_two, f_six = swap(f_own, 2), swap(f_own, 6)
    f_top, f_low = swap(f_six[:half], 2), swap(f_two[half:], 6)
    here = [f_own, f_two, f_six, f_top, f_low]
    factors = here + [swap(part, 1) for part in here]
    delta = pl.pallas_call(
        functools.partial(lab_kernel, slots, rows),
        out_shape=shape_of((col_tiles, lab_share, rank), bf16),
        in_specs=[SMEM] + [ANY] * (2 + len(pieces) + len(factors) + 3),
        out_specs=VMEM,
        scratch_shapes=[
            pltpu.VMEM((rows, 2 * slots + 1, lab_share, size), bf16),
            pltpu.VMEM((rows * tiles, size, rank), bf16),
            pltpu.VMEM((col_tiles, lab_share, rank), bf16),
            pltpu.VMEM((col_tiles, lab_share, rank), f32),
            pltpu.VMEM((col_tiles, lab_share, rank), bf16),
            pltpu.VMEM((col_tiles, lab_share, size), f32),
            pltpu.SemaphoreType.DMA((rows,)),
            pltpu.SemaphoreType.DMA((rows,)),
            pltpu.SemaphoreType.DMA,
            pltpu.VMEM((rows, lab_share, size), bf16),
            pltpu.VMEM((rows, size), jnp.int32),
            pltpu.SMEM((rows, size), jnp.int32),
            pltpu.SemaphoreType.DMA((rows,)),
            pltpu.SemaphoreType.DMA,
        ],
        compiler_params=params(BIG),
        name="lab_step",
    )(row, same[0], other, *pieces, *factors, labs, late_here, late_there)
    back = lax.all_to_all(
        delta.reshape(col_tiles * lab_share, rank), "rows", split_axis=0, concat_axis=0, tiled=True
    )
    back = back.reshape(rows, owned_tiles, lab_share, rank).transpose(1, 0, 2, 3)
    own_labs = jnp.concatenate([own, late_here[:, 0]], axis=1)
    updated = own_labs.reshape(owned_tiles, rows, lab_share, rank).astype(f32) + back.astype(f32)
    return (patient_out, updated.reshape(1, owned_tiles * size, rank))


def solution(mesh):
    in_specs = (
        P(("rows", "cols"), None),
        P("rows", None),
        P("rows", "cols", None, None),
        P("rows", "cols", None, None),
        P("rows", "cols"),
        P("rows", "cols"),
        P("rows", "cols"),
        P("rows", None),
        P(),
    )
    out_specs = (P(("rows", "cols"), None), P("cols", "rows", None))
    return jax.shard_map(shards, mesh=mesh, in_specs=in_specs, out_specs=out_specs, check_vma=False)
```

```python
import functools

import jax
import jax.numpy as jnp
from jax import lax
from jax.experimental import pallas as pl
from jax.experimental.pallas import tpu as pltpu
from jax.sharding import PartitionSpec as P

ITERS = 3
ridge_term = 1.0
highest = lax.Precision.HIGHEST
bf16 = jnp.bfloat16
f32 = jnp.float32
MIB = 1 << 20
BIG = 56

VMEM = pl.BlockSpec(memory_space=pltpu.VMEM)
SMEM = pl.BlockSpec(memory_space=pltpu.SMEM)
ANY = pl.BlockSpec(memory_space=pl.ANY)

GROUP = 8
CHUNK = 6
LAB_CHUNK = 8
SIDE = 4
PASS_TYPES = (f32, bf16)


def dot_nt(a, b):
    return lax.dot_general(a, b, (((1,), (1,)), ((), ())), preferred_element_type=f32)


def dot_nn(a, b):
    return lax.dot_general(a, b, (((1,), (0,)), ((), ())), preferred_element_type=f32)


def prep_kernel(
    tiles, slots, row_ref, patient_ref, lab_ref, count_ref, x_any, w_any, meta_ref, work_ref, xs_any, ws_any, *rest
):
    x_ref, w_ref, tmp, order, fill, x_sem, w_sem, xs_sem, ws_sem = rest[-9:]
    same, other = rest[:-10], rest[-10]
    n = 2 * len(same)
    pieces = [same[k // 2] if k % 2 == 0 else other.at[k // 2] for k in range(n)]
    share = x_any.shape[2] // n
    live = count_ref[0, 0]
    row = row_ref[0]

    def clear(i, carry):
        meta_ref[0, i] = 0
        return carry

    lax.fori_loop(0, meta_ref.shape[1], clear, 0)
    for p in range(tiles + 2):
        fill[p] = 0

    def key_of(s):
        return jnp.where(s < live, patient_ref[0, s], tiles)

    def count(s, carry):
        key = key_of(s)
        fill[key + 1] = fill[key + 1] + 1
        return carry

    lax.fori_loop(0, slots, count, 0)
    for p in range(tiles + 1):
        fill[p + 1] = fill[p + 1] + fill[p]
        meta_ref[0, slots + p] = fill[p]

    def place(s, carry):
        key = key_of(s)
        at = fill[key]
        fill[key] = at + 1
        order[at] = s
        meta_ref[0, at] = lab_ref[0, s]
        return carry

    lax.fori_loop(0, slots, place, 0)

    def at(c):
        return pl.ds(c * GROUP, GROUP)

    def fetch(c, carry):
        for j in range(GROUP):
            s = c * GROUP + j
            pltpu.make_async_copy(x_any.at[order[s]], x_ref.at[s], x_sem.at[c]).start()
            pltpu.make_async_copy(w_any.at[order[s]], w_ref.at[s], w_sem.at[c]).start()
        return carry

    lax.fori_loop(0, slots // GROUP, fetch, 0)

    def hand_on(c):
        return (
            pltpu.make_async_copy(x_ref.at[at(c)], xs_any.at[at(c)], xs_sem.at[c]),
            pltpu.make_async_copy(w_ref.at[at(c)], ws_any.at[at(c)], ws_sem.at[c]),
        )

    def no_work(i, carry):
        for f in range(4):
            work_ref[f, i] = 0
        return carry

    lax.fori_loop(0, work_ref.shape[1], no_work, 0)
    chunks = jnp.int32(0)
    for p in range(tiles):
        lo, hi = meta_ref[0, slots + p], meta_ref[0, slots + p + 1]

        def add(i, carry, p=p, lo=lo, hi=hi, chunks=chunks):
            work_ref[0, chunks + i] = p
            work_ref[1, chunks + i] = lo + i * CHUNK
            work_ref[2, chunks + i] = hi
            return carry

        count_p = (hi - lo + CHUNK - 1) // CHUNK
        lax.fori_loop(0, count_p, add, 0)
        chunks = chunks + count_p

    def pad(i, carry):
        work_ref[2, i] = live
        work_ref[1, i] = live
        return carry

    blocks = (chunks + SIDE - 1) // SIDE
    lax.fori_loop(chunks, blocks * SIDE, pad, 0)
    work_ref[3, 0] = blocks

    lane = lax.broadcasted_iota(jnp.int32, (share, meta_ref.shape[1]), 1)
    table = jnp.zeros(lane.shape, f32)
    for i in range(slots + tiles + 1):
        table = jnp.where(lane == i, meta_ref[0, i].astype(f32), table)
    for k in range(n):
        pieces[k][2 * slots] = table.astype(bf16)

    size = x_any.shape[1]
    eye = (
        lax.broadcasted_iota(jnp.int32, (size, size), 0)
        == lax.broadcasted_iota(jnp.int32, (size, size), 1)
    ).astype(f32).astype(bf16)

    def turn(c, carry):
        pltpu.make_async_copy(x_any.at[at(c)], x_ref.at[at(c)], x_sem.at[c]).wait()
        pltpu.make_async_copy(w_any.at[at(c)], w_ref.at[at(c)], w_sem.at[c]).wait()
        for copy in hand_on(c):
            copy.start()
        for u in range(GROUP):
            tmp[u, 0] = dot_nt(eye, x_ref[c * GROUP + u]).astype(bf16)
            tmp[u, 1] = dot_nt(eye, w_ref[c * GROUP + u]).astype(bf16)
        for u in range(GROUP):
            s = c * GROUP + u
            for k in range(n):
                rows = pl.ds(pl.multiple_of((row ^ k) * share, share), share)
                pieces[k][s] = tmp[u, 0, rows, :]
                pieces[k][slots + s] = tmp[u, 1, rows, :]
        return carry

    lax.fori_loop(0, slots // GROUP, turn, 0)

    def end(c, carry):
        for copy in hand_on(c):
            copy.wait()
        return carry

    lax.fori_loop(0, slots // GROUP, end, 0)


def patient_sums(with_values, work_ref, x_ref, w_ref, v_ref, t_ref, y_ref, out_ref, acc, arrive):
    acc[...] = jnp.zeros_like(acc)

    def chunk(c):
        tile, first, end = [work_ref[f, c] for f in range(3)]
        at = [jnp.maximum(jnp.minimum(first + j, end - 1), 0) for j in range(CHUNK)]
        labs = jnp.concatenate([v_ref[a] for a in at], axis=0)
        turned = jnp.concatenate([t_ref[a] for a in at], axis=1)
        wts = jnp.concatenate(
            [w_ref[a].astype(f32) * (first + j < end).astype(f32) for j, a in enumerate(at)], axis=1
        )
        scores = dot_nn(y_ref[tile], turned)
        if with_values:
            vals = jnp.concatenate([x_ref[a].astype(f32) for a in at], axis=1)
            kern = wts * (vals - scores)
        else:
            kern = wts * scores
        return tile, dot_nn(kern.astype(bf16), labs)

    def block(b, there):
        there = arrive(there, work_ref[2, b * SIDE + SIDE - 1])
        found = [chunk(b * SIDE + j) for j in range(SIDE)]
        for tile, terms in found:
            acc[tile] += terms
        return there

    lax.fori_loop(0, work_ref[3, 0], block, jnp.int32(1))
    out_ref[...] = acc[...].astype(out_ref.dtype)


def first_pass_kernel(
    slots, n, row_ref, meta_ref, work_ref, xs_any, ws_any, y_ref, early_any, here_any, there_any, *refs
):
    out_ref, kept_any, turned_any, v_ref, w_ref, x_ref, acc, v_sem, w_sem, x_sem, kept_sem = refs[:11]
    t_ref, turned_sem = refs[11:]
    row = row_ref[0]
    live = meta_ref[0, slots + y_ref.shape[0]]
    batches = (live + GROUP - 1) // GROUP
    owned = early_any.shape[0] // n
    early = early_any.shape[1]
    late = v_ref.shape[1] - early

    def at(c):
        return pl.ds(c * GROUP, GROUP)

    def rest(c):
        return (
            pltpu.make_async_copy(ws_any.at[at(c)], w_ref.at[at(c)], w_sem.at[c]),
            pltpu.make_async_copy(xs_any.at[at(c)], x_ref.at[at(c)], x_sem.at[c]),
        )

    def keep(c):
        return (
            pltpu.make_async_copy(v_ref.at[at(c)], kept_any.at[at(c)], kept_sem.at[c]),
            pltpu.make_async_copy(t_ref.at[at(c)], turned_any.at[at(c)], turned_sem.at[c]),
        )

    def start(c, carry):
        for j in range(GROUP):
            s = c * GROUP + j
            tile = meta_ref[0, s]
            source = row ^ (tile // owned)
            pltpu.make_async_copy(
                early_any.at[tile], v_ref.at[s, pl.ds(0, early), :], v_sem.at[c]
            ).start()
            for core, late_any in enumerate((here_any, there_any)):

                @pl.when(source % 2 == core)
                def _(late_any=late_any, s=s, tile=tile, source=source):
                    pltpu.make_async_copy(
                        late_any.at[tile % owned, source // 2],
                        v_ref.at[s, pl.ds(early, late), :],
                        v_sem.at[c],
                    ).start()

        for copy in rest(c):
            copy.start()
        return carry

    lax.fori_loop(0, batches, start, 0)

    def wait(c, carry):
        for copy in rest(c):
            copy.wait()
        pltpu.make_async_copy(kept_any.at[at(c)], v_ref.at[at(c)], v_sem.at[c]).wait()
        for j in range(GROUP):
            t_ref[c * GROUP + j] = v_ref[c * GROUP + j].T
        for copy in keep(c):
            copy.start()
        return carry

    wait(0, 0)

    def arrive(there, hi):
        until = jnp.maximum((hi + GROUP - 1) // GROUP, there)
        lax.fori_loop(there, until, wait, 0)
        return until

    patient_sums(True, work_ref, x_ref, w_ref, v_ref, t_ref, y_ref, out_ref, acc, arrive)

    def end(c, carry):
        for copy in keep(c):
            copy.wait()
        return carry

    lax.fori_loop(0, batches, end, 0)


def pass_kernel(
    slots, meta_ref, work_ref, w_ref, kept_any, turned_any, y_ref, out_ref, v_ref, t_ref, acc, v_sem, t_sem
):
    batches = (meta_ref[0, slots + y_ref.shape[0]] + GROUP - 1) // GROUP

    def copies(c):
        at = pl.ds(c * GROUP, GROUP)
        return (
            pltpu.make_async_copy(turned_any.at[at], t_ref.at[at], t_sem.at[c]),
            pltpu.make_async_copy(kept_any.at[at], v_ref.at[at], v_sem.at[c]),
        )

    def start(c, carry):
        for copy in copies(c):
            copy.start()
        return carry

    def wait(c, carry):
        for copy in copies(c):
            copy.wait()
        return carry

    lax.fori_loop(0, batches, start, 0)
    wait(0, 0)

    def arrive(there, hi):
        until = jnp.maximum((hi + GROUP - 1) // GROUP, there)
        lax.fori_loop(there, until, wait, 0)
        return until

    patient_sums(False, work_ref, None, w_ref, v_ref, t_ref, y_ref, out_ref, acc, arrive)


def spread(probe_ref, rows):
    for k in range(probe_ref.shape[0]):
        probe_ref[k] = rows


def first_kernel(recv_ref, start_ref, side_ref, gram_ref, state_ref, probe_ref):
    residual = jnp.sum(recv_ref[...].astype(f32), axis=0) + side_ref[...]
    state_ref[0] = start_ref[...].astype(f32)
    state_ref[1] = residual
    state_ref[2] = residual
    state_ref[3] = (
        jnp.dot(residual, gram_ref[...], precision=highest, preferred_element_type=f32)
        + ridge_term * residual
    )
    spread(probe_ref, residual.astype(bf16))


def step_kernel(turn_ref, recv_ref, state_in, gram_ref, state_ref, probe_ref):
    residual = state_in[1]
    direction = state_in[2]
    applied = jnp.sum(recv_ref[...].astype(f32), axis=0) + state_in[3]
    norm_now = jnp.sum(residual * residual, axis=1, keepdims=True)
    step_size = norm_now / jnp.sum(direction * applied, axis=1, keepdims=True)
    solution_now = state_in[0] + step_size * direction
    state_ref[0] = solution_now
    last = turn_ref[0] == ITERS - 1

    @pl.when(last)
    def _():
        spread(probe_ref, solution_now.astype(bf16))

    @pl.when(jnp.logical_not(last))
    def _():
        residual_next = residual - step_size * applied
        norm_next = jnp.sum(residual_next * residual_next, axis=1, keepdims=True)
        direction_next = residual_next + norm_next / norm_now * direction
        state_ref[1] = residual_next
        state_ref[2] = direction_next
        state_ref[3] = (
            jnp.dot(
                direction_next, gram_ref[...], precision=highest, preferred_element_type=f32
            )
            + ridge_term * direction_next
        )
        spread(probe_ref, direction_next.astype(bf16))


def lab_kernel(slots, n, row_ref, same_any, other_any, *refs):
    pieces = [same_any, other_any.at[0]]
    for ref in refs[: n // 2 - 1]:
        pieces += [ref.at[0], ref.at[1]]
    refs = refs[n // 2 - 1 :]
    f_own, f_two, f_six, f_top, f_low, g_own, g_two, g_six, g_top, g_low = refs[:10]
    early_any, here_any, there_any, out_ref, xw, f_ref, v_ref, acc, probe, curv, p_sem, f_sem, v_sem = refs[10:23]
    coded, table, meta_ref, t_sem, m_sem = refs[23:]
    tiles = f_ref.shape[0] // n
    half = tiles // 2
    share = v_ref.shape[1]
    size = f_ref.shape[1]
    row = row_ref[0]
    t_copies = [
        pltpu.make_async_copy(pieces[k].at[2 * slots], coded.at[k], t_sem.at[k]) for k in range(n)
    ]
    for copy in t_copies:
        copy.start()
    early = early_any.shape[1] // share
    owned = v_ref.shape[0] // n

    @pl.when(row < early)
    def _():
        at = pl.ds(row * share, share)
        pltpu.make_async_copy(early_any.at[:, at, :], v_ref, v_sem).start()

    @pl.when(row >= early)
    def _():
        at = pl.ds((row - early) * share, share)
        for k in range(n):
            part = (here_any, there_any)[k % 2].at[:, k // 2, at, :]
            to = pl.ds((row ^ k) * owned, owned)
            pltpu.make_async_copy(part, v_ref.at[to], v_sem).start()

    factors = {0: [f_own], 1: [g_own], 2: [f_two], 3: [g_two], 6: [f_six], 7: [g_six]}
    factors |= {4: [f_top, f_low], 5: [g_top, g_low]}
    for k in range(n):
        pltpu.make_async_copy(pieces[k], xw.at[k], p_sem.at[k]).start()
        for h, ref in enumerate(factors[k]):
            to = pl.ds((row ^ k) * tiles + h * half, ref.shape[0])
            pltpu.make_async_copy(ref, f_ref.at[to], f_sem.at[k]).start()
    for k, copy in enumerate(t_copies):
        copy.wait()
        table[k : k + 1] = coded[k, 0:1].astype(f32).astype(jnp.int32)
    m_copy = pltpu.make_async_copy(table, meta_ref, m_sem)
    m_copy.start()
    acc[...] = jnp.zeros_like(acc)
    curv[...] = jnp.zeros_like(curv)
    m_copy.wait()
    pltpu.make_async_copy(v_ref, v_ref, v_sem).wait()

    span = LAB_CHUNK * share
    row_slot = lax.broadcasted_iota(jnp.int32, (span, size), 0) // share

    def sweep(terms_of, total, arrive):
        def of_source(k, carry):
            source = row ^ k
            arrive(k, source)
            lo = [meta_ref[k, slots + p] for p in range(tiles)]
            hi = [meta_ref[k, slots + p + 1] for p in range(tiles)]

            def block(i, carry):
                found = []
                for p in range(tiles):
                    first = lo[p] + i * LAB_CHUNK
                    base = jnp.minimum(first, slots - LAB_CHUNK)
                    labs = [meta_ref[k, base + j] for j in range(LAB_CHUNK)]
                    inside = (row_slot >= first - base) & (row_slot < hi[p] - base)
                    wts = xw[k, pl.ds(slots + base, LAB_CHUNK)].reshape(span, size).astype(f32)
                    wts = jnp.where(inside, wts, 0.0)
                    found.append((labs, terms_of(k, base, labs, wts, f_ref[source * tiles + p])))
                for labs, terms in found:
                    for j, t in enumerate(labs):
                        total[t] += terms[j * share : (j + 1) * share]
                return carry

            most = functools.reduce(jnp.maximum, [b - a for a, b in zip(lo, hi)])
            return lax.fori_loop(0, (most + LAB_CHUNK - 1) // LAB_CHUNK, block, carry)

        lax.fori_loop(0, n, of_source, 0)

    def residual_terms(k, base, labs, wts, patients):
        rows = jnp.concatenate([v_ref[t] for t in labs], axis=0)
        vals = xw[k, pl.ds(base, LAB_CHUNK)].reshape(span, size).astype(f32)
        return dot_nn((wts * (vals - dot_nt(rows, patients))).astype(bf16), patients)

    def arrive(k, source):
        pltpu.make_async_copy(xw.at[0], xw.at[k], p_sem.at[k]).wait()
        at = pl.ds(source * tiles, tiles)
        pltpu.make_async_copy(f_ref.at[pl.ds(0, tiles)], f_ref.at[at], f_sem.at[k]).wait()

    sweep(residual_terms, acc, arrive)

    block = 16

    def finish(i, carry):
        at = pl.ds(i * block, block)
        rest = acc[at] - ridge_term * v_ref[at].astype(f32)
        acc[at] = rest
        probe[at] = rest.astype(bf16)
        return carry

    lax.fori_loop(0, acc.shape[0] // block, finish, 0)

    def curvature_terms(k, base, labs, wts, patients):
        rows = jnp.concatenate([probe[t] for t in labs], axis=0)
        inner = dot_nt(rows, patients)
        return wts * inner * inner

    sweep(curvature_terms, curv, lambda k, source: None)

    def emit(i, carry):
        at = pl.ds(i * block, block)
        rest = acc[at]
        norm = jnp.sum(rest * rest, axis=-1, keepdims=True)
        total = jnp.sum(curv[at], axis=-1, keepdims=True) + ridge_term * norm
        out_ref[at] = (norm / total * rest).astype(out_ref.dtype)
        return carry

    lax.fori_loop(0, acc.shape[0] // block, emit, 0)


def shape_of(shape, dtype):
    return jax.ShapeDtypeStruct(shape, dtype)


def params(mib):
    return pltpu.CompilerParams(vmem_limit_bytes=mib * MIB)


def shards(
    lab_factors,
    patient_factors,
    values,
    weights,
    tile_patient,
    tile_lab,
    tile_count,
    ecg_embed,
    ecg_map,
):
    rows = lax.axis_size("rows")
    cols = lax.axis_size("cols")
    size = values.shape[2]
    slots = values.shape[1]
    rank = lab_factors.shape[1]
    owned_tiles = lab_factors.shape[0] // size
    col_tiles = owned_tiles * rows
    patient_rows = patient_factors.shape[0]
    tiles = patient_rows // size
    share_rows = patient_rows // cols
    lab_share = size // rows
    row = lax.axis_index("rows").astype(jnp.int32).reshape(1)
    x, w = values[0], weights[0]

    def swap(array, k):
        return lax.ppermute(array, "rows", [(i, i ^ k) for i in range(rows)])

    def to_columns(array):
        return lax.all_to_all(array, "cols", split_axis=0, concat_axis=0, tiled=True)

    slot_shape = shape_of((slots, size, size), bf16)
    piece = (2 * slots + 1, lab_share, size)
    out_pieces = [shape_of(piece, bf16)] * (rows // 2) + [shape_of((rows // 2, *piece), bf16)]
    prep = pl.pallas_call(
        functools.partial(prep_kernel, tiles, slots),
        out_shape=[shape_of((1, 128), jnp.int32), shape_of((4, 128), jnp.int32)]
        + [slot_shape] * 2
        + out_pieces,
        in_specs=[SMEM] * 4 + [ANY] * 2,
        out_specs=[SMEM] * 2 + [ANY] * 2 + [VMEM] * len(out_pieces),
        scratch_shapes=[
            pltpu.VMEM((slots, size, size), bf16),
            pltpu.VMEM((slots, size, size), bf16),
            pltpu.VMEM((GROUP, 2, size, size), bf16),
            pltpu.SMEM((slots,), jnp.int32),
            pltpu.SMEM((tiles + 2,), jnp.int32),
        ]
        + [pltpu.SemaphoreType.DMA((slots // GROUP,))] * 4,
        compiler_params=params(BIG),
        cost_estimate=pl.CostEstimate(flops=10**9, bytes_accessed=48 * MIB, transcendentals=0),
        name="prep",
    )(row, tile_patient, tile_lab, tile_count, x, w)
    (meta, work, xs, ws), same, other = prep[:4], prep[4:-1], prep[-1]

    early = size - size // 4
    given = lab_factors.reshape(owned_tiles, size, rank)
    late = given[:, early:]
    late = [late] + [swap(late, 2 * h) for h in range(1, rows // 2)]
    own = to_columns(given[:, :early])
    labs = lax.all_gather(own, "rows", axis=0, tiled=True)
    late, _ = lax.optimization_barrier((late, own))
    late_here = to_columns(jnp.stack(late, axis=1))
    late_there = swap(late_here, 1)
    other = swap(other, 1)

    embed_map = ecg_map.astype(f32)
    gram = jnp.dot(embed_map.T, embed_map, precision=highest)
    share_at = lax.axis_index("cols") * share_rows
    start_share = lax.dynamic_slice_in_dim(patient_factors, share_at, share_rows).astype(f32)
    embed_share = lax.dynamic_slice_in_dim(ecg_embed, share_at, share_rows).astype(f32)
    side = (
        jnp.dot(
            embed_share - jnp.dot(start_share, embed_map.T, precision=highest),
            embed_map,
            precision=highest,
        )
        - ridge_term * start_share
    )

    labs, late_here, late_there, same, other = lax.optimization_barrier(
        (labs, late_here, late_there, same, other)
    )
    pieces = [jnp.stack([same[h], other[h]]) for h in range(1, rows // 2)]
    pieces = [swap(piece, 2 * h) for h, piece in enumerate(pieces, 1)]

    def exchange(partial):
        partial = partial.reshape(patient_rows, rank)
        recv = lax.all_to_all(partial, "cols", split_axis=0, concat_axis=0, tiled=True)
        return recv.reshape(cols, share_rows, rank)

    def to_all(probe):
        probe = probe.reshape(patient_rows, rank)
        probe = lax.all_to_all(probe, "cols", split_axis=0, concat_axis=0, tiled=True)
        return probe.reshape(tiles, size, rank)

    state_shape = shape_of((4, share_rows, rank), f32)
    probe_shape = shape_of((cols, share_rows, rank), bf16)
    batches = slots // GROUP
    partial, slot_labs, turned_labs = pl.pallas_call(
        functools.partial(first_pass_kernel, slots, rows),
        out_shape=[
            shape_of((tiles, size, rank), PASS_TYPES[0]),
            shape_of((slots, size, rank), bf16),
            shape_of((slots, rank, size), bf16),
        ],
        in_specs=[SMEM] * 3 + [VMEM] * 3 + [ANY] * 3,
        out_specs=[VMEM, ANY, ANY],
        scratch_shapes=[
            pltpu.VMEM((slots, size, rank), bf16),
            pltpu.VMEM((slots, size, size), bf16),
            pltpu.VMEM((slots, size, size), bf16),
            pltpu.VMEM((tiles, size, rank), f32),
        ]
        + [pltpu.SemaphoreType.DMA((batches,))] * 4
        + [pltpu.VMEM((slots, rank, size), bf16), pltpu.SemaphoreType.DMA((batches,))],
        compiler_params=params(BIG),
        name="first_pass",
    )(
        row,
        meta,
        work,
        xs,
        ws,
        patient_factors.reshape(tiles, size, rank),
        labs,
        late_here,
        late_there,
    )
    state, probe = pl.pallas_call(
        first_kernel,
        out_shape=[state_shape, probe_shape],
        in_specs=[VMEM] * 4,
        out_specs=[VMEM] * 2,
        compiler_params=params(8),
        name="first_step",
    )(exchange(partial), start_share, side, gram)

    def turn(iteration, carry):
        state, probe = carry
        partial = pl.pallas_call(
            functools.partial(pass_kernel, slots),
            out_shape=shape_of((tiles, size, rank), PASS_TYPES[1]),
            in_specs=[SMEM] * 2 + [VMEM, ANY, ANY, VMEM],
            out_specs=VMEM,
            scratch_shapes=[
                pltpu.VMEM((slots, size, rank), bf16),
                pltpu.VMEM((slots, rank, size), bf16),
                pltpu.VMEM((tiles, size, rank), f32),
                pltpu.SemaphoreType.DMA((batches,)),
                pltpu.SemaphoreType.DMA((batches,)),
            ],
            compiler_params=params(28),
            name="patient_pass",
        )(meta, work, ws, slot_labs, turned_labs, to_all(probe))
        state, probe = pl.pallas_call(
            step_kernel,
            out_shape=[state_shape, probe_shape],
            in_specs=[SMEM] + [VMEM] * 3,
            out_specs=[VMEM] * 2,
            compiler_params=params(8),
            name="step",
        )(iteration.reshape(1), exchange(partial), state, gram)
        return state, probe

    state, probe = lax.fori_loop(0, ITERS, turn, (state, probe))
    patient_out = state[0]

    f_own = to_all(probe)
    half = tiles // 2
    f_two, f_six = swap(f_own, 2), swap(f_own, 6)
    f_top, f_low = swap(f_six[:half], 2), swap(f_two[half:], 6)
    here = [f_own, f_two, f_six, f_top, f_low]
    factors = here + [swap(part, 1) for part in here]
    delta = pl.pallas_call(
        functools.partial(lab_kernel, slots, rows),
        out_shape=shape_of((col_tiles, lab_share, rank), bf16),
        in_specs=[SMEM] + [ANY] * (2 + len(pieces) + len(factors) + 3),
        out_specs=VMEM,
        scratch_shapes=[
            pltpu.VMEM((rows, 2 * slots + 1, lab_share, size), bf16),
            pltpu.VMEM((rows * tiles, size, rank), bf16),
            pltpu.VMEM((col_tiles, lab_share, rank), bf16),
            pltpu.VMEM((col_tiles, lab_share, rank), f32),
            pltpu.VMEM((col_tiles, lab_share, rank), bf16),
            pltpu.VMEM((col_tiles, lab_share, size), f32),
            pltpu.SemaphoreType.DMA((rows,)),
            pltpu.SemaphoreType.DMA((rows,)),
            pltpu.SemaphoreType.DMA,
            pltpu.VMEM((rows, lab_share, size), bf16),
            pltpu.VMEM((rows, size), jnp.int32),
            pltpu.SMEM((rows, size), jnp.int32),
            pltpu.SemaphoreType.DMA((rows,)),
            pltpu.SemaphoreType.DMA,
        ],
        compiler_params=params(BIG),
        name="lab_step",
    )(row, same[0], other, *pieces, *factors, labs, late_here, late_there)
    back = lax.all_to_all(
        delta.reshape(col_tiles * lab_share, rank), "rows", split_axis=0, concat_axis=0, tiled=True
    )
    back = back.reshape(rows, owned_tiles, lab_share, rank).transpose(1, 0, 2, 3)
    own_labs = jnp.concatenate([own, late_here[:, 0]], axis=1)
    updated = own_labs.reshape(owned_tiles, rows, lab_share, rank).astype(f32) + back.astype(f32)
    return (patient_out, updated.reshape(1, owned_tiles * size, rank))


def solution(mesh):
    in_specs = (
        P(("rows", "cols"), None),
        P("rows", None),
        P("rows", "cols", None, None),
        P("rows", "cols", None, None),
        P("rows", "cols"),
        P("rows", "cols"),
        P("rows", "cols"),
        P("rows", None),
        P(),
    )
    out_specs = (P(("rows", "cols"), None), P("cols", "rows", None))
    return jax.shard_map(shards, mesh=mesh, in_specs=in_specs, out_specs=out_specs, check_vma=False)
```

```python
import functools

import jax
import jax.numpy as jnp
from jax import lax
from jax.experimental import pallas as pl
from jax.experimental.pallas import tpu as pltpu
from jax.sharding import PartitionSpec as P

ITERS = 3
ridge_term = 1.0
highest = lax.Precision.HIGHEST
bf16 = jnp.bfloat16
f32 = jnp.float32
MIB = 1 << 20
BIG = 56

VMEM = pl.BlockSpec(memory_space=pltpu.VMEM)
SMEM = pl.BlockSpec(memory_space=pltpu.SMEM)
ANY = pl.BlockSpec(memory_space=pl.ANY)

GROUP = 8
CHUNK = 6
LAB_CHUNK = 8
SIDE = 5
PASS_TYPES = (f32, bf16)


def dot_nt(a, b):
    return lax.dot_general(a, b, (((1,), (1,)), ((), ())), preferred_element_type=f32)


def dot_nn(a, b):
    return lax.dot_general(a, b, (((1,), (0,)), ((), ())), preferred_element_type=f32)


def prep_kernel(
    tiles, slots, row_ref, patient_ref, lab_ref, count_ref, x_any, w_any, meta_ref, work_ref, xs_any, ws_any, *rest
):
    x_ref, w_ref, tmp, order, fill, x_sem, w_sem, xs_sem, ws_sem = rest[-9:]
    same, other = rest[:-10], rest[-10]
    n = 2 * len(same)
    pieces = [same[k // 2] if k % 2 == 0 else other.at[k // 2] for k in range(n)]
    share = x_any.shape[2] // n
    live = count_ref[0, 0]
    row = row_ref[0]

    def clear(i, carry):
        meta_ref[0, i] = 0
        return carry

    lax.fori_loop(0, meta_ref.shape[1], clear, 0)
    for p in range(tiles + 2):
        fill[p] = 0

    def key_of(s):
        return jnp.where(s < live, patient_ref[0, s], tiles)

    def count(s, carry):
        key = key_of(s)
        fill[key + 1] = fill[key + 1] + 1
        return carry

    lax.fori_loop(0, slots, count, 0)
    for p in range(tiles + 1):
        fill[p + 1] = fill[p + 1] + fill[p]
        meta_ref[0, slots + p] = fill[p]

    def place(s, carry):
        key = key_of(s)
        at = fill[key]
        fill[key] = at + 1
        order[at] = s
        meta_ref[0, at] = lab_ref[0, s]
        return carry

    lax.fori_loop(0, slots, place, 0)

    def at(c):
        return pl.ds(c * GROUP, GROUP)

    def fetch(c, carry):
        for j in range(GROUP):
            s = c * GROUP + j
            pltpu.make_async_copy(x_any.at[order[s]], x_ref.at[s], x_sem.at[c]).start()
            pltpu.make_async_copy(w_any.at[order[s]], w_ref.at[s], w_sem.at[c]).start()
        return carry

    lax.fori_loop(0, slots // GROUP, fetch, 0)

    def hand_on(c):
        return (
            pltpu.make_async_copy(x_ref.at[at(c)], xs_any.at[at(c)], xs_sem.at[c]),
            pltpu.make_async_copy(w_ref.at[at(c)], ws_any.at[at(c)], ws_sem.at[c]),
        )

    def no_work(i, carry):
        for f in range(4):
            work_ref[f, i] = 0
        return carry

    lax.fori_loop(0, work_ref.shape[1], no_work, 0)
    chunks = jnp.int32(0)
    for p in range(tiles):
        lo, hi = meta_ref[0, slots + p], meta_ref[0, slots + p + 1]

        def add(i, carry, p=p, lo=lo, hi=hi, chunks=chunks):
            work_ref[0, chunks + i] = p
            work_ref[1, chunks + i] = lo + i * CHUNK
            work_ref[2, chunks + i] = hi
            return carry

        count_p = (hi - lo + CHUNK - 1) // CHUNK
        lax.fori_loop(0, count_p, add, 0)
        chunks = chunks + count_p

    def pad(i, carry):
        work_ref[2, i] = live
        work_ref[1, i] = live
        return carry

    blocks = (chunks + SIDE - 1) // SIDE
    lax.fori_loop(chunks, blocks * SIDE, pad, 0)
    work_ref[3, 0] = blocks

    lane = lax.broadcasted_iota(jnp.int32, (share, meta_ref.shape[1]), 1)
    table = jnp.zeros(lane.shape, f32)
    for i in range(slots + tiles + 1):
        table = jnp.where(lane == i, meta_ref[0, i].astype(f32), table)
    for k in range(n):
        pieces[k][2 * slots] = table.astype(bf16)

    size = x_any.shape[1]
    eye = (
        lax.broadcasted_iota(jnp.int32, (size, size), 0)
        == lax.broadcasted_iota(jnp.int32, (size, size), 1)
    ).astype(f32).astype(bf16)

    def turn(c, carry):
        pltpu.make_async_copy(x_any.at[at(c)], x_ref.at[at(c)], x_sem.at[c]).wait()
        pltpu.make_async_copy(w_any.at[at(c)], w_ref.at[at(c)], w_sem.at[c]).wait()
        for copy in hand_on(c):
            copy.start()
        for u in range(GROUP):
            tmp[u, 0] = dot_nt(eye, x_ref[c * GROUP + u]).astype(bf16)
            tmp[u, 1] = dot_nt(eye, w_ref[c * GROUP + u]).astype(bf16)
        for u in range(GROUP):
            s = c * GROUP + u
            for k in range(n):
                rows = pl.ds(pl.multiple_of((row ^ k) * share, share), share)
                pieces[k][s] = tmp[u, 0, rows, :]
                pieces[k][slots + s] = tmp[u, 1, rows, :]
        return carry

    lax.fori_loop(0, slots // GROUP, turn, 0)

    def end(c, carry):
        for copy in hand_on(c):
            copy.wait()
        return carry

    lax.fori_loop(0, slots // GROUP, end, 0)


def patient_sums(with_values, work_ref, x_ref, w_ref, v_ref, t_ref, y_ref, out_ref, acc, arrive):
    acc[...] = jnp.zeros_like(acc)

    def chunk(c):
        tile, first, end = [work_ref[f, c] for f in range(3)]
        at = [jnp.maximum(jnp.minimum(first + j, end - 1), 0) for j in range(CHUNK)]
        labs = jnp.concatenate([v_ref[a] for a in at], axis=0)
        turned = jnp.concatenate([t_ref[a] for a in at], axis=1)
        wts = jnp.concatenate(
            [w_ref[a].astype(f32) * (first + j < end).astype(f32) for j, a in enumerate(at)], axis=1
        )
        scores = dot_nn(y_ref[tile], turned)
        if with_values:
            vals = jnp.concatenate([x_ref[a].astype(f32) for a in at], axis=1)
            kern = wts * (vals - scores)
        else:
            kern = wts * scores
        return tile, dot_nn(kern.astype(bf16), labs)

    def block(b, there):
        there = arrive(there, work_ref[2, b * SIDE + SIDE - 1])
        found = [chunk(b * SIDE + j) for j in range(SIDE)]
        for tile, terms in found:
            acc[tile] += terms
        return there

    lax.fori_loop(0, work_ref[3, 0], block, jnp.int32(1))
    out_ref[...] = acc[...].astype(out_ref.dtype)


def first_pass_kernel(
    slots, n, row_ref, meta_ref, work_ref, xs_any, ws_any, y_ref, early_any, here_any, there_any, *refs
):
    out_ref, kept_any, turned_any, v_ref, w_ref, x_ref, acc, v_sem, w_sem, x_sem, kept_sem = refs[:11]
    t_ref, turned_sem = refs[11:]
    row = row_ref[0]
    live = meta_ref[0, slots + y_ref.shape[0]]
    batches = (live + GROUP - 1) // GROUP
    owned = early_any.shape[0] // n
    early = early_any.shape[1]
    late = v_ref.shape[1] - early

    def at(c):
        return pl.ds(c * GROUP, GROUP)

    def rest(c):
        return (
            pltpu.make_async_copy(ws_any.at[at(c)], w_ref.at[at(c)], w_sem.at[c]),
            pltpu.make_async_copy(xs_any.at[at(c)], x_ref.at[at(c)], x_sem.at[c]),
        )

    def keep(c):
        return (
            pltpu.make_async_copy(v_ref.at[at(c)], kept_any.at[at(c)], kept_sem.at[c]),
            pltpu.make_async_copy(t_ref.at[at(c)], turned_any.at[at(c)], turned_sem.at[c]),
        )

    def start(c, carry):
        for j in range(GROUP):
            s = c * GROUP + j
            tile = meta_ref[0, s]
            source = row ^ (tile // owned)
            pltpu.make_async_copy(
                early_any.at[tile], v_ref.at[s, pl.ds(0, early), :], v_sem.at[c]
            ).start()
            for core, late_any in enumerate((here_any, there_any)):

                @pl.when(source % 2 == core)
                def _(late_any=late_any, s=s, tile=tile, source=source):
                    pltpu.make_async_copy(
                        late_any.at[tile % owned, source // 2],
                        v_ref.at[s, pl.ds(early, late), :],
                        v_sem.at[c],
                    ).start()

        for copy in rest(c):
            copy.start()
        return carry

    lax.fori_loop(0, batches, start, 0)

    def wait(c, carry):
        for copy in rest(c):
            copy.wait()
        pltpu.make_async_copy(kept_any.at[at(c)], v_ref.at[at(c)], v_sem.at[c]).wait()
        for j in range(GROUP):
            t_ref[c * GROUP + j] = v_ref[c * GROUP + j].T
        for copy in keep(c):
            copy.start()
        return carry

    wait(0, 0)

    def arrive(there, hi):
        until = jnp.maximum((hi + GROUP - 1) // GROUP, there)
        lax.fori_loop(there, until, wait, 0)
        return until

    patient_sums(True, work_ref, x_ref, w_ref, v_ref, t_ref, y_ref, out_ref, acc, arrive)

    def end(c, carry):
        for copy in keep(c):
            copy.wait()
        return carry

    lax.fori_loop(0, batches, end, 0)


def pass_kernel(slots, meta_ref, work_ref, ws_any, kept_any, turned_any, y_ref, out_ref, *refs):
    w_ref, v_ref, t_ref, acc, w_sem, v_sem, t_sem = refs
    batches = (meta_ref[0, slots + y_ref.shape[0]] + GROUP - 1) // GROUP

    def copies(c):
        at = pl.ds(c * GROUP, GROUP)
        return (
            pltpu.make_async_copy(ws_any.at[at], w_ref.at[at], w_sem.at[c]),
            pltpu.make_async_copy(turned_any.at[at], t_ref.at[at], t_sem.at[c]),
            pltpu.make_async_copy(kept_any.at[at], v_ref.at[at], v_sem.at[c]),
        )

    def start(c, carry):
        for copy in copies(c):
            copy.start()
        return carry

    def wait(c, carry):
        for copy in copies(c):
            copy.wait()
        return carry

    lax.fori_loop(0, batches, start, 0)
    wait(0, 0)

    def arrive(there, hi):
        until = jnp.maximum((hi + GROUP - 1) // GROUP, there)
        lax.fori_loop(there, until, wait, 0)
        return until

    patient_sums(False, work_ref, None, w_ref, v_ref, t_ref, y_ref, out_ref, acc, arrive)


def spread(probe_ref, rows):
    for k in range(probe_ref.shape[0]):
        probe_ref[k] = rows


def first_kernel(recv_ref, start_ref, side_ref, gram_ref, state_ref, probe_ref):
    residual = jnp.sum(recv_ref[...].astype(f32), axis=0) + side_ref[...]
    state_ref[0] = start_ref[...].astype(f32)
    state_ref[1] = residual
    state_ref[2] = residual
    state_ref[3] = (
        jnp.dot(residual, gram_ref[...], precision=highest, preferred_element_type=f32)
        + ridge_term * residual
    )
    spread(probe_ref, residual.astype(bf16))


def step_kernel(turn_ref, recv_ref, state_in, gram_ref, state_ref, probe_ref):
    residual = state_in[1]
    direction = state_in[2]
    applied = jnp.sum(recv_ref[...].astype(f32), axis=0) + state_in[3]
    norm_now = jnp.sum(residual * residual, axis=1, keepdims=True)
    step_size = norm_now / jnp.sum(direction * applied, axis=1, keepdims=True)
    solution_now = state_in[0] + step_size * direction
    state_ref[0] = solution_now
    last = turn_ref[0] == ITERS - 1

    @pl.when(last)
    def _():
        spread(probe_ref, solution_now.astype(bf16))

    @pl.when(jnp.logical_not(last))
    def _():
        residual_next = residual - step_size * applied
        norm_next = jnp.sum(residual_next * residual_next, axis=1, keepdims=True)
        direction_next = residual_next + norm_next / norm_now * direction
        state_ref[1] = residual_next
        state_ref[2] = direction_next
        state_ref[3] = (
            jnp.dot(
                direction_next, gram_ref[...], precision=highest, preferred_element_type=f32
            )
            + ridge_term * direction_next
        )
        spread(probe_ref, direction_next.astype(bf16))


def lab_kernel(slots, n, row_ref, same_any, other_any, *refs):
    pieces = [same_any, other_any.at[0]]
    for ref in refs[: n // 2 - 1]:
        pieces += [ref.at[0], ref.at[1]]
    refs = refs[n // 2 - 1 :]
    f_own, f_two, f_six, f_top, f_low, g_own, g_two, g_six, g_top, g_low = refs[:10]
    early_any, here_any, there_any, out_ref, xw, f_ref, v_ref, acc, probe, curv, p_sem, f_sem, v_sem = refs[10:23]
    coded, table, meta_ref, t_sem, m_sem = refs[23:]
    tiles = f_ref.shape[0] // n
    half = tiles // 2
    share = v_ref.shape[1]
    size = f_ref.shape[1]
    row = row_ref[0]
    t_copies = [
        pltpu.make_async_copy(pieces[k].at[2 * slots], coded.at[k], t_sem.at[k]) for k in range(n)
    ]
    for copy in t_copies:
        copy.start()
    early = early_any.shape[1] // share
    owned = v_ref.shape[0] // n

    @pl.when(row < early)
    def _():
        at = pl.ds(row * share, share)
        pltpu.make_async_copy(early_any.at[:, at, :], v_ref, v_sem).start()

    @pl.when(row >= early)
    def _():
        at = pl.ds((row - early) * share, share)
        for k in range(n):
            part = (here_any, there_any)[k % 2].at[:, k // 2, at, :]
            to = pl.ds((row ^ k) * owned, owned)
            pltpu.make_async_copy(part, v_ref.at[to], v_sem).start()

    factors = {0: [f_own], 1: [g_own], 2: [f_two], 3: [g_two], 6: [f_six], 7: [g_six]}
    factors |= {4: [f_top, f_low], 5: [g_top, g_low]}
    for k in range(n):
        pltpu.make_async_copy(pieces[k], xw.at[k], p_sem.at[k]).start()
        for h, ref in enumerate(factors[k]):
            to = pl.ds((row ^ k) * tiles + h * half, ref.shape[0])
            pltpu.make_async_copy(ref, f_ref.at[to], f_sem.at[k]).start()
    for k, copy in enumerate(t_copies):
        copy.wait()
        table[k : k + 1] = coded[k].astype(f32).astype(jnp.int32)[0:1]
    m_copy = pltpu.make_async_copy(table, meta_ref, m_sem)
    m_copy.start()
    acc[...] = jnp.zeros_like(acc)
    curv[...] = jnp.zeros_like(curv)
    m_copy.wait()
    pltpu.make_async_copy(v_ref, v_ref, v_sem).wait()

    span = LAB_CHUNK * share
    row_slot = lax.broadcasted_iota(jnp.int32, (span, size), 0) // share

    def sweep(terms_of, total, arrive):
        def of_source(k, carry):
            source = row ^ k
            arrive(k, source)
            lo = [meta_ref[k, slots + p] for p in range(tiles)]
            hi = [meta_ref[k, slots + p + 1] for p in range(tiles)]

            def block(i, carry):
                found = []
                for p in range(tiles):
                    first = lo[p] + i * LAB_CHUNK
                    base = jnp.minimum(first, slots - LAB_CHUNK)
                    labs = [meta_ref[k, base + j] for j in range(LAB_CHUNK)]
                    inside = (row_slot >= first - base) & (row_slot < hi[p] - base)
                    wts = xw[k, pl.ds(slots + base, LAB_CHUNK)].reshape(span, size).astype(f32)
                    wts = jnp.where(inside, wts, 0.0)
                    found.append((labs, terms_of(k, base, labs, wts, f_ref[source * tiles + p])))
                for labs, terms in found:
                    for j, t in enumerate(labs):
                        total[t] += terms[j * share : (j + 1) * share]
                return carry

            most = functools.reduce(jnp.maximum, [b - a for a, b in zip(lo, hi)])
            return lax.fori_loop(0, (most + LAB_CHUNK - 1) // LAB_CHUNK, block, carry)

        lax.fori_loop(0, n, of_source, 0)

    def residual_terms(k, base, labs, wts, patients):
        rows = jnp.concatenate([v_ref[t] for t in labs], axis=0)
        vals = xw[k, pl.ds(base, LAB_CHUNK)].reshape(span, size).astype(f32)
        return dot_nn((wts * (vals - dot_nt(rows, patients))).astype(bf16), patients)

    def arrive(k, source):
        pltpu.make_async_copy(xw.at[0], xw.at[k], p_sem.at[k]).wait()
        at = pl.ds(source * tiles, tiles)
        pltpu.make_async_copy(f_ref.at[pl.ds(0, tiles)], f_ref.at[at], f_sem.at[k]).wait()

    sweep(residual_terms, acc, arrive)

    block = 16

    def finish(i, carry):
        at = pl.ds(i * block, block)
        rest = acc[at] - ridge_term * v_ref[at].astype(f32)
        acc[at] = rest
        probe[at] = rest.astype(bf16)
        return carry

    lax.fori_loop(0, acc.shape[0] // block, finish, 0)

    def curvature_terms(k, base, labs, wts, patients):
        rows = jnp.concatenate([probe[t] for t in labs], axis=0)
        inner = dot_nt(rows, patients)
        return wts * inner * inner

    sweep(curvature_terms, curv, lambda k, source: None)

    def emit(i, carry):
        at = pl.ds(i * block, block)
        rest = acc[at]
        norm = jnp.sum(rest * rest, axis=-1, keepdims=True)
        total = jnp.sum(curv[at], axis=-1, keepdims=True) + ridge_term * norm
        out_ref[at] = (norm / total * rest).astype(out_ref.dtype)
        return carry

    lax.fori_loop(0, acc.shape[0] // block, emit, 0)


def shape_of(shape, dtype):
    return jax.ShapeDtypeStruct(shape, dtype)


def params(mib):
    return pltpu.CompilerParams(vmem_limit_bytes=mib * MIB)


def shards(
    lab_factors,
    patient_factors,
    values,
    weights,
    tile_patient,
    tile_lab,
    tile_count,
    ecg_embed,
    ecg_map,
):
    rows = lax.axis_size("rows")
    cols = lax.axis_size("cols")
    size = values.shape[2]
    slots = values.shape[1]
    rank = lab_factors.shape[1]
    owned_tiles = lab_factors.shape[0] // size
    col_tiles = owned_tiles * rows
    patient_rows = patient_factors.shape[0]
    tiles = patient_rows // size
    share_rows = patient_rows // cols
    lab_share = size // rows
    row = lax.axis_index("rows").astype(jnp.int32).reshape(1)
    x, w = values[0], weights[0]

    def swap(array, k):
        return lax.ppermute(array, "rows", [(i, i ^ k) for i in range(rows)])

    def to_columns(array):
        return lax.all_to_all(array, "cols", split_axis=0, concat_axis=0, tiled=True)

    slot_shape = shape_of((slots, size, size), bf16)
    piece = (2 * slots + 1, lab_share, size)
    out_pieces = [shape_of(piece, bf16)] * (rows // 2) + [shape_of((rows // 2, *piece), bf16)]
    prep = pl.pallas_call(
        functools.partial(prep_kernel, tiles, slots),
        out_shape=[shape_of((1, 128), jnp.int32), shape_of((4, 128), jnp.int32)]
        + [slot_shape] * 2
        + out_pieces,
        in_specs=[SMEM] * 4 + [ANY] * 2,
        out_specs=[SMEM] * 2 + [ANY] * 2 + [VMEM] * len(out_pieces),
        scratch_shapes=[
            pltpu.VMEM((slots, size, size), bf16),
            pltpu.VMEM((slots, size, size), bf16),
            pltpu.VMEM((GROUP, 2, size, size), bf16),
            pltpu.SMEM((slots,), jnp.int32),
            pltpu.SMEM((tiles + 2,), jnp.int32),
        ]
        + [pltpu.SemaphoreType.DMA((slots // GROUP,))] * 4,
        compiler_params=params(BIG),
        cost_estimate=pl.CostEstimate(flops=10**9, bytes_accessed=48 * MIB, transcendentals=0),
        name="prep",
    )(row, tile_patient, tile_lab, tile_count, x, w)
    (meta, work, xs, ws), same, other = prep[:4], prep[4:-1], prep[-1]

    early = size - size // 4
    given = lab_factors.reshape(owned_tiles, size, rank)
    late = given[:, early:]
    late = [late] + [swap(late, 2 * h) for h in range(1, rows // 2)]
    own = to_columns(given[:, :early])
    labs = lax.all_gather(own, "rows", axis=0, tiled=True)
    late, _ = lax.optimization_barrier((late, own))
    late_here = to_columns(jnp.stack(late, axis=1))
    late_there = swap(late_here, 1)
    other = swap(other, 1)

    embed_map = ecg_map.astype(f32)
    gram = jnp.dot(embed_map.T, embed_map, precision=highest)
    share_at = lax.axis_index("cols") * share_rows
    start_share = lax.dynamic_slice_in_dim(patient_factors, share_at, share_rows).astype(f32)
    embed_share = lax.dynamic_slice_in_dim(ecg_embed, share_at, share_rows).astype(f32)
    side = (
        jnp.dot(
            embed_share - jnp.dot(start_share, embed_map.T, precision=highest),
            embed_map,
            precision=highest,
        )
        - ridge_term * start_share
    )

    labs, late_here, late_there, same, other = lax.optimization_barrier(
        (labs, late_here, late_there, same, other)
    )
    pieces = [jnp.stack([same[h], other[h]]) for h in range(1, rows // 2)]
    pieces = [swap(piece, 2 * h) for h, piece in enumerate(pieces, 1)]
    own_labs = jnp.concatenate([own, late_here[:, 0]], axis=1)

    def exchange(partial):
        partial = partial.reshape(patient_rows, rank)
        recv = lax.all_to_all(partial, "cols", split_axis=0, concat_axis=0, tiled=True)
        return recv.reshape(cols, share_rows, rank)

    def to_all(probe):
        probe = probe.reshape(patient_rows, rank)
        probe = lax.all_to_all(probe, "cols", split_axis=0, concat_axis=0, tiled=True)
        return probe.reshape(tiles, size, rank)

    state_shape = shape_of((4, share_rows, rank), f32)
    probe_shape = shape_of((cols, share_rows, rank), bf16)
    batches = slots // GROUP
    partial, slot_labs, turned_labs = pl.pallas_call(
        functools.partial(first_pass_kernel, slots, rows),
        out_shape=[
            shape_of((tiles, size, rank), PASS_TYPES[0]),
            shape_of((slots, size, rank), bf16),
            shape_of((slots, rank, size), bf16),
        ],
        in_specs=[SMEM] * 3 + [VMEM] * 3 + [ANY] * 3,
        out_specs=[VMEM, ANY, ANY],
        scratch_shapes=[
            pltpu.VMEM((slots, size, rank), bf16),
            pltpu.VMEM((slots, size, size), bf16),
            pltpu.VMEM((slots, size, size), bf16),
            pltpu.VMEM((tiles, size, rank), f32),
        ]
        + [pltpu.SemaphoreType.DMA((batches,))] * 4
        + [pltpu.VMEM((slots, rank, size), bf16), pltpu.SemaphoreType.DMA((batches,))],
        compiler_params=params(BIG),
        name="first_pass",
    )(
        row,
        meta,
        work,
        xs,
        ws,
        patient_factors.reshape(tiles, size, rank),
        labs,
        late_here,
        late_there,
    )
    state, probe = pl.pallas_call(
        first_kernel,
        out_shape=[state_shape, probe_shape],
        in_specs=[VMEM] * 4,
        out_specs=[VMEM] * 2,
        compiler_params=params(8),
        name="first_step",
    )(exchange(partial), start_share, side, gram)

    def turn(iteration, carry):
        state, probe = carry
        partial = pl.pallas_call(
            functools.partial(pass_kernel, slots),
            out_shape=shape_of((tiles, size, rank), PASS_TYPES[1]),
            in_specs=[SMEM] * 2 + [ANY] * 3 + [VMEM],
            out_specs=VMEM,
            scratch_shapes=[
                pltpu.VMEM((slots, size, size), bf16),
                pltpu.VMEM((slots, size, rank), bf16),
                pltpu.VMEM((slots, rank, size), bf16),
                pltpu.VMEM((tiles, size, rank), f32),
                pltpu.SemaphoreType.DMA((batches,)),
                pltpu.SemaphoreType.DMA((batches,)),
                pltpu.SemaphoreType.DMA((batches,)),
            ],
            compiler_params=params(28),
            name="patient_pass",
        )(meta, work, ws, slot_labs, turned_labs, to_all(probe))
        state, probe = pl.pallas_call(
            step_kernel,
            out_shape=[state_shape, probe_shape],
            in_specs=[SMEM] + [VMEM] * 3,
            out_specs=[VMEM] * 2,
            compiler_params=params(8),
            name="step",
        )(iteration.reshape(1), exchange(partial), state, gram)
        return state, probe

    own_labs, state, probe = lax.optimization_barrier((own_labs, state, probe))
    state, probe = lax.fori_loop(0, ITERS, turn, (state, probe))
    patient_out = state[0]

    f_own = to_all(probe)
    half = tiles // 2
    f_two, f_six = swap(f_own, 2), swap(f_own, 6)
    f_top, f_low = swap(f_six[:half], 2), swap(f_two[half:], 6)
    here = [f_own, f_two, f_six, f_top, f_low]
    factors = here + [swap(part, 1) for part in here]
    delta = pl.pallas_call(
        functools.partial(lab_kernel, slots, rows),
        out_shape=shape_of((col_tiles, lab_share, rank), bf16),
        in_specs=[SMEM] + [ANY] * (2 + len(pieces) + len(factors) + 3),
        out_specs=VMEM,
        scratch_shapes=[
            pltpu.VMEM((rows, 2 * slots + 1, lab_share, size), bf16),
            pltpu.VMEM((rows * tiles, size, rank), bf16),
            pltpu.VMEM((col_tiles, lab_share, rank), bf16),
            pltpu.VMEM((col_tiles, lab_share, rank), f32),
            pltpu.VMEM((col_tiles, lab_share, rank), bf16),
            pltpu.VMEM((col_tiles, lab_share, size), f32),
            pltpu.SemaphoreType.DMA((rows,)),
            pltpu.SemaphoreType.DMA((rows,)),
            pltpu.SemaphoreType.DMA,
            pltpu.VMEM((rows, lab_share, size), bf16),
            pltpu.VMEM((rows, size), jnp.int32),
            pltpu.SMEM((rows, size), jnp.int32),
            pltpu.SemaphoreType.DMA((rows,)),
            pltpu.SemaphoreType.DMA,
        ],
        compiler_params=params(44),
        name="lab_step",
    )(row, same[0], other, *pieces, *factors, labs, late_here, late_there)
    back = lax.all_to_all(
        delta.reshape(col_tiles * lab_share, rank), "rows", split_axis=0, concat_axis=0, tiled=True
    )
    back = back.reshape(rows, owned_tiles, lab_share, rank).transpose(1, 0, 2, 3)
    updated = own_labs.reshape(owned_tiles, rows, lab_share, rank).astype(f32) + back.astype(f32)
    return (patient_out, updated.reshape(1, owned_tiles * size, rank))


def solution(mesh):
    in_specs = (
        P(("rows", "cols"), None),
        P("rows", None),
        P("rows", "cols", None, None),
        P("rows", "cols", None, None),
        P("rows", "cols"),
        P("rows", "cols"),
        P("rows", "cols"),
        P("rows", None),
        P(),
    )
    out_specs = (P(("rows", "cols"), None), P("cols", "rows", None))
    return jax.shard_map(shards, mesh=mesh, in_specs=in_specs, out_specs=out_specs, check_vma=False)
```

```python
import functools

import jax
import jax.numpy as jnp
from jax import lax
from jax.experimental import pallas as pl
from jax.experimental.pallas import tpu as pltpu
from jax.sharding import PartitionSpec as P

ITERS = 3
ridge_term = 1.0
highest = lax.Precision.HIGHEST
bf16 = jnp.bfloat16
f32 = jnp.float32
MIB = 1 << 20
BIG = 56

VMEM = pl.BlockSpec(memory_space=pltpu.VMEM)
SMEM = pl.BlockSpec(memory_space=pltpu.SMEM)
ANY = pl.BlockSpec(memory_space=pl.ANY)

GROUP = 8
CHUNK = 6
LAB_CHUNK = 8
SIDE = 5
PASS_TYPES = (f32, bf16)


def dot_nt(a, b):
    return lax.dot_general(a, b, (((1,), (1,)), ((), ())), preferred_element_type=f32)


def dot_nn(a, b):
    return lax.dot_general(a, b, (((1,), (0,)), ((), ())), preferred_element_type=f32)


def prep_kernel(
    tiles, slots, row_ref, patient_ref, lab_ref, count_ref, x_any, w_any, meta_ref, work_ref, xs_any, ws_any, *rest
):
    x_ref, w_ref, tmp, order, fill, x_sem, w_sem, xs_sem, ws_sem = rest[-9:]
    same, other = rest[:-10], rest[-10]
    n = 2 * len(same)
    pieces = [same[k // 2] if k % 2 == 0 else other.at[k // 2] for k in range(n)]
    share = x_any.shape[2] // n
    live = count_ref[0, 0]
    row = row_ref[0]

    def clear(i, carry):
        meta_ref[0, i] = 0
        return carry

    lax.fori_loop(0, meta_ref.shape[1], clear, 0)
    for p in range(tiles + 2):
        fill[p] = 0

    def key_of(s):
        return jnp.where(s < live, patient_ref[0, s], tiles)

    def count(s, carry):
        key = key_of(s)
        fill[key + 1] = fill[key + 1] + 1
        return carry

    lax.fori_loop(0, slots, count, 0)
    for p in range(tiles + 1):
        fill[p + 1] = fill[p + 1] + fill[p]
        meta_ref[0, slots + p] = fill[p]

    def place(s, carry):
        key = key_of(s)
        at = fill[key]
        fill[key] = at + 1
        order[at] = s
        meta_ref[0, at] = lab_ref[0, s]
        return carry

    lax.fori_loop(0, slots, place, 0)

    def at(c):
        return pl.ds(c * GROUP, GROUP)

    def fetch(c, carry):
        for j in range(GROUP):
            s = c * GROUP + j
            pltpu.make_async_copy(x_any.at[order[s]], x_ref.at[s], x_sem.at[c]).start()
            pltpu.make_async_copy(w_any.at[order[s]], w_ref.at[s], w_sem.at[c]).start()
        return carry

    lax.fori_loop(0, slots // GROUP, fetch, 0)

    def hand_on(c):
        return (
            pltpu.make_async_copy(x_ref.at[at(c)], xs_any.at[at(c)], xs_sem.at[c]),
            pltpu.make_async_copy(w_ref.at[at(c)], ws_any.at[at(c)], ws_sem.at[c]),
        )

    def no_work(i, carry):
        for f in range(4):
            work_ref[f, i] = 0
        return carry

    lax.fori_loop(0, work_ref.shape[1], no_work, 0)
    chunks = jnp.int32(0)
    for p in range(tiles):
        lo, hi = meta_ref[0, slots + p], meta_ref[0, slots + p + 1]

        def add(i, carry, p=p, lo=lo, hi=hi, chunks=chunks):
            work_ref[0, chunks + i] = p
            work_ref[1, chunks + i] = lo + i * CHUNK
            work_ref[2, chunks + i] = hi
            return carry

        count_p = (hi - lo + CHUNK - 1) // CHUNK
        lax.fori_loop(0, count_p, add, 0)
        chunks = chunks + count_p

    def pad(i, carry):
        work_ref[2, i] = live
        work_ref[1, i] = live
        return carry

    blocks = (chunks + SIDE - 1) // SIDE
    lax.fori_loop(chunks, blocks * SIDE, pad, 0)
    work_ref[3, 0] = blocks

    lane = lax.broadcasted_iota(jnp.int32, (share, meta_ref.shape[1]), 1)
    table = jnp.zeros(lane.shape, f32)
    for i in range(slots + tiles + 1):
        table = jnp.where(lane == i, meta_ref[0, i].astype(f32), table)
    for k in range(n):
        pieces[k][2 * slots] = table.astype(bf16)

    size = x_any.shape[1]
    eye = (
        lax.broadcasted_iota(jnp.int32, (size, size), 0)
        == lax.broadcasted_iota(jnp.int32, (size, size), 1)
    ).astype(f32).astype(bf16)

    def turn(c, carry):
        pltpu.make_async_copy(x_any.at[at(c)], x_ref.at[at(c)], x_sem.at[c]).wait()
        pltpu.make_async_copy(w_any.at[at(c)], w_ref.at[at(c)], w_sem.at[c]).wait()
        for copy in hand_on(c):
            copy.start()
        for u in range(GROUP):
            tmp[u, 0] = dot_nt(eye, x_ref[c * GROUP + u]).astype(bf16)
            tmp[u, 1] = dot_nt(eye, w_ref[c * GROUP + u]).astype(bf16)
        for u in range(GROUP):
            s = c * GROUP + u
            for k in range(n):
                rows = pl.ds(pl.multiple_of((row ^ k) * share, share), share)
                pieces[k][s] = tmp[u, 0, rows, :]
                pieces[k][slots + s] = tmp[u, 1, rows, :]
        return carry

    lax.fori_loop(0, slots // GROUP, turn, 0)

    def end(c, carry):
        for copy in hand_on(c):
            copy.wait()
        return carry

    lax.fori_loop(0, slots // GROUP, end, 0)


def patient_sums(with_values, work_ref, x_ref, w_ref, v_ref, t_ref, y_ref, out_ref, acc, arrive):

    def chunk(c):
        tile, first, end = [work_ref[f, c] for f in range(3)]
        at = [jnp.maximum(jnp.minimum(first + j, end - 1), 0) for j in range(CHUNK)]
        labs = jnp.concatenate([v_ref[a] for a in at], axis=0)
        turned = jnp.concatenate([t_ref[a] for a in at], axis=1)
        wts = jnp.concatenate(
            [w_ref[a].astype(f32) * (first + j < end).astype(f32) for j, a in enumerate(at)], axis=1
        )
        scores = dot_nn(y_ref[tile], turned)
        if with_values:
            vals = jnp.concatenate([x_ref[a].astype(f32) for a in at], axis=1)
            kern = wts * (vals - scores)
        else:
            kern = wts * scores
        return tile, dot_nn(kern.astype(bf16), labs)

    def block(b, there):
        there = arrive(there, work_ref[2, b * SIDE + SIDE - 1])
        found = [chunk(b * SIDE + j) for j in range(SIDE)]
        for tile, terms in found:
            acc[tile] += terms
        return there

    lax.fori_loop(0, work_ref[3, 0], block, jnp.int32(1))
    out_ref[...] = acc[...].astype(out_ref.dtype)


def first_pass_kernel(
    slots, n, row_ref, meta_ref, work_ref, xs_any, ws_any, y_ref, early_any, here_any, there_any, *refs
):
    out_ref, kept_any, turned_any, v_ref, w_ref, x_ref, acc, v_sem, w_sem, x_sem, kept_sem = refs[:11]
    t_ref, turned_sem = refs[11:]
    row = row_ref[0]
    live = meta_ref[0, slots + y_ref.shape[0]]
    batches = (live + GROUP - 1) // GROUP
    owned = early_any.shape[0] // n
    early = early_any.shape[1]
    late = v_ref.shape[1] - early

    def at(c):
        return pl.ds(c * GROUP, GROUP)

    def rest(c):
        return (
            pltpu.make_async_copy(ws_any.at[at(c)], w_ref.at[at(c)], w_sem.at[c]),
            pltpu.make_async_copy(xs_any.at[at(c)], x_ref.at[at(c)], x_sem.at[c]),
        )

    def keep(c):
        return (
            pltpu.make_async_copy(v_ref.at[at(c)], kept_any.at[at(c)], kept_sem.at[c]),
            pltpu.make_async_copy(t_ref.at[at(c)], turned_any.at[at(c)], turned_sem.at[c]),
        )

    def start(c, carry):
        for j in range(GROUP):
            s = c * GROUP + j
            tile = meta_ref[0, s]
            source = row ^ (tile // owned)
            pltpu.make_async_copy(
                early_any.at[tile], v_ref.at[s, pl.ds(0, early), :], v_sem.at[c]
            ).start()
            for core, late_any in enumerate((here_any, there_any)):

                @pl.when(source % 2 == core)
                def _(late_any=late_any, s=s, tile=tile, source=source):
                    pltpu.make_async_copy(
                        late_any.at[tile % owned, source // 2],
                        v_ref.at[s, pl.ds(early, late), :],
                        v_sem.at[c],
                    ).start()

        for copy in rest(c):
            copy.start()
        return carry

    lax.fori_loop(0, batches, start, 0)

    def wait(c, carry):
        for copy in rest(c):
            copy.wait()
        pltpu.make_async_copy(kept_any.at[at(c)], v_ref.at[at(c)], v_sem.at[c]).wait()
        for j in range(GROUP):
            t_ref[c * GROUP + j] = v_ref[c * GROUP + j].T
        for copy in keep(c):
            copy.start()
        return carry

    acc[...] = jnp.zeros_like(acc)
    wait(0, 0)

    def arrive(there, hi):
        until = jnp.maximum((hi + GROUP - 1) // GROUP, there)
        lax.fori_loop(there, until, wait, 0)
        return until

    patient_sums(True, work_ref, x_ref, w_ref, v_ref, t_ref, y_ref, out_ref, acc, arrive)

    def end(c, carry):
        for copy in keep(c):
            copy.wait()
        return carry

    lax.fori_loop(0, batches, end, 0)


def pass_kernel(slots, meta_ref, work_ref, ws_any, kept_any, turned_any, y_ref, out_ref, *refs):
    w_ref, v_ref, t_ref, acc, w_sem, v_sem, t_sem = refs
    batches = (meta_ref[0, slots + y_ref.shape[0]] + GROUP - 1) // GROUP

    def copies(c):
        at = pl.ds(c * GROUP, GROUP)
        return (
            pltpu.make_async_copy(ws_any.at[at], w_ref.at[at], w_sem.at[c]),
            pltpu.make_async_copy(turned_any.at[at], t_ref.at[at], t_sem.at[c]),
            pltpu.make_async_copy(kept_any.at[at], v_ref.at[at], v_sem.at[c]),
        )

    def start(c, carry):
        for copy in copies(c):
            copy.start()
        return carry

    def wait(c, carry):
        for copy in copies(c):
            copy.wait()
        return carry

    lax.fori_loop(0, batches, start, 0)
    acc[...] = jnp.zeros_like(acc)
    wait(0, 0)

    def arrive(there, hi):
        until = jnp.maximum((hi + GROUP - 1) // GROUP, there)
        lax.fori_loop(there, until, wait, 0)
        return until

    patient_sums(False, work_ref, None, w_ref, v_ref, t_ref, y_ref, out_ref, acc, arrive)


def spread(probe_ref, rows):
    for k in range(probe_ref.shape[0]):
        probe_ref[k] = rows


def first_kernel(recv_ref, start_ref, side_ref, gram_ref, state_ref, probe_ref):
    residual = jnp.sum(recv_ref[...].astype(f32), axis=0) + side_ref[...]
    state_ref[0] = start_ref[...].astype(f32)
    state_ref[1] = residual
    state_ref[2] = residual
    state_ref[3] = (
        jnp.dot(residual, gram_ref[...], precision=highest, preferred_element_type=f32)
        + ridge_term * residual
    )
    spread(probe_ref, residual.astype(bf16))


def step_kernel(turn_ref, recv_ref, state_in, gram_ref, state_ref, probe_ref):
    residual = state_in[1]
    direction = state_in[2]
    applied = jnp.sum(recv_ref[...].astype(f32), axis=0) + state_in[3]
    norm_now = jnp.sum(residual * residual, axis=1, keepdims=True)
    step_size = norm_now / jnp.sum(direction * applied, axis=1, keepdims=True)
    solution_now = state_in[0] + step_size * direction
    state_ref[0] = solution_now
    last = turn_ref[0] == ITERS - 1

    @pl.when(last)
    def _():
        spread(probe_ref, solution_now.astype(bf16))

    @pl.when(jnp.logical_not(last))
    def _():
        residual_next = residual - step_size * applied
        norm_next = jnp.sum(residual_next * residual_next, axis=1, keepdims=True)
        direction_next = residual_next + norm_next / norm_now * direction
        state_ref[1] = residual_next
        state_ref[2] = direction_next
        state_ref[3] = (
            jnp.dot(
                direction_next, gram_ref[...], precision=highest, preferred_element_type=f32
            )
            + ridge_term * direction_next
        )
        spread(probe_ref, direction_next.astype(bf16))


def lab_kernel(slots, n, row_ref, same_any, other_any, *refs):
    pieces = [same_any, other_any.at[0]]
    for ref in refs[: n // 2 - 1]:
        pieces += [ref.at[0], ref.at[1]]
    refs = refs[n // 2 - 1 :]
    f_own, f_two, f_six, f_top, f_low, g_own, g_two, g_six, g_top, g_low = refs[:10]
    early_any, here_any, there_any, out_ref, xw, f_ref, v_ref, acc, probe, curv, p_sem, f_sem, v_sem = refs[10:23]
    coded, table, meta_ref, t_sem, m_sem = refs[23:]
    tiles = f_ref.shape[0] // n
    half = tiles // 2
    share = v_ref.shape[1]
    size = f_ref.shape[1]
    row = row_ref[0]
    t_copies = [
        pltpu.make_async_copy(pieces[k].at[2 * slots], coded.at[k], t_sem.at[k]) for k in range(n)
    ]
    for copy in t_copies:
        copy.start()
    early = early_any.shape[1] // share
    owned = v_ref.shape[0] // n

    @pl.when(row < early)
    def _():
        at = pl.ds(row * share, share)
        pltpu.make_async_copy(early_any.at[:, at, :], v_ref, v_sem).start()

    @pl.when(row >= early)
    def _():
        at = pl.ds((row - early) * share, share)
        for k in range(n):
            part = (here_any, there_any)[k % 2].at[:, k // 2, at, :]
            to = pl.ds((row ^ k) * owned, owned)
            pltpu.make_async_copy(part, v_ref.at[to], v_sem).start()

    factors = {0: [f_own], 1: [g_own], 2: [f_two], 3: [g_two], 6: [f_six], 7: [g_six]}
    factors |= {4: [f_top, f_low], 5: [g_top, g_low]}
    for k in range(n):
        pltpu.make_async_copy(pieces[k], xw.at[k], p_sem.at[k]).start()
        for h, ref in enumerate(factors[k]):
            to = pl.ds((row ^ k) * tiles + h * half, ref.shape[0])
            pltpu.make_async_copy(ref, f_ref.at[to], f_sem.at[k]).start()
    acc[...] = jnp.zeros_like(acc)
    for k, copy in enumerate(t_copies):
        copy.wait()
        table[k : k + 1] = coded[k].astype(f32).astype(jnp.int32)[0:1]
    m_copy = pltpu.make_async_copy(table, meta_ref, m_sem)
    m_copy.start()
    curv[...] = jnp.zeros_like(curv)
    m_copy.wait()
    pltpu.make_async_copy(v_ref, v_ref, v_sem).wait()

    span = LAB_CHUNK * share
    row_slot = lax.broadcasted_iota(jnp.int32, (span, size), 0) // share

    def sweep(terms_of, total, arrive):
        def of_source(k, carry):
            source = row ^ k
            arrive(k, source)
            lo = [meta_ref[k, slots + p] for p in range(tiles)]
            hi = [meta_ref[k, slots + p + 1] for p in range(tiles)]

            def block(i, carry):
                found = []
                for p in range(tiles):
                    first = lo[p] + i * LAB_CHUNK
                    base = jnp.minimum(first, slots - LAB_CHUNK)
                    labs = [meta_ref[k, base + j] for j in range(LAB_CHUNK)]
                    inside = (row_slot >= first - base) & (row_slot < hi[p] - base)
                    wts = xw[k, pl.ds(slots + base, LAB_CHUNK)].reshape(span, size).astype(f32)
                    wts = jnp.where(inside, wts, 0.0)
                    found.append((labs, terms_of(k, base, labs, wts, f_ref[source * tiles + p])))
                for labs, terms in found:
                    for j, t in enumerate(labs):
                        total[t] += terms[j * share : (j + 1) * share]
                return carry

            most = functools.reduce(jnp.maximum, [b - a for a, b in zip(lo, hi)])
            return lax.fori_loop(0, (most + LAB_CHUNK - 1) // LAB_CHUNK, block, carry)

        lax.fori_loop(0, n, of_source, 0)

    def residual_terms(k, base, labs, wts, patients):
        rows = jnp.concatenate([v_ref[t] for t in labs], axis=0)
        vals = xw[k, pl.ds(base, LAB_CHUNK)].reshape(span, size).astype(f32)
        return dot_nn((wts * (vals - dot_nt(rows, patients))).astype(bf16), patients)

    def arrive(k, source):
        pltpu.make_async_copy(xw.at[0], xw.at[k], p_sem.at[k]).wait()
        at = pl.ds(source * tiles, tiles)
        pltpu.make_async_copy(f_ref.at[pl.ds(0, tiles)], f_ref.at[at], f_sem.at[k]).wait()

    sweep(residual_terms, acc, arrive)

    block = 16

    def finish(i, carry):
        at = pl.ds(i * block, block)
        rest = acc[at] - ridge_term * v_ref[at].astype(f32)
        acc[at] = rest
        probe[at] = rest.astype(bf16)
        return carry

    lax.fori_loop(0, acc.shape[0] // block, finish, 0)

    def curvature_terms(k, base, labs, wts, patients):
        rows = jnp.concatenate([probe[t] for t in labs], axis=0)
        inner = dot_nt(rows, patients)
        return wts * inner * inner

    sweep(curvature_terms, curv, lambda k, source: None)

    def emit(i, carry):
        at = pl.ds(i * block, block)
        rest = acc[at]
        norm = jnp.sum(rest * rest, axis=-1, keepdims=True)
        total = jnp.sum(curv[at], axis=-1, keepdims=True) + ridge_term * norm
        out_ref[at] = (norm / total * rest).astype(out_ref.dtype)
        return carry

    lax.fori_loop(0, acc.shape[0] // block, emit, 0)


def shape_of(shape, dtype):
    return jax.ShapeDtypeStruct(shape, dtype)


def params(mib):
    return pltpu.CompilerParams(vmem_limit_bytes=mib * MIB)


def shards(
    lab_factors,
    patient_factors,
    values,
    weights,
    tile_patient,
    tile_lab,
    tile_count,
    ecg_embed,
    ecg_map,
):
    rows = lax.axis_size("rows")
    cols = lax.axis_size("cols")
    size = values.shape[2]
    slots = values.shape[1]
    rank = lab_factors.shape[1]
    owned_tiles = lab_factors.shape[0] // size
    col_tiles = owned_tiles * rows
    patient_rows = patient_factors.shape[0]
    tiles = patient_rows // size
    share_rows = patient_rows // cols
    lab_share = size // rows
    row = lax.axis_index("rows").astype(jnp.int32).reshape(1)
    x, w = values[0], weights[0]

    def swap(array, k):
        return lax.ppermute(array, "rows", [(i, i ^ k) for i in range(rows)])

    def to_columns(array):
        return lax.all_to_all(array, "cols", split_axis=0, concat_axis=0, tiled=True)

    slot_shape = shape_of((slots, size, size), bf16)
    piece = (2 * slots + 1, lab_share, size)
    out_pieces = [shape_of(piece, bf16)] * (rows // 2) + [shape_of((rows // 2, *piece), bf16)]
    prep = pl.pallas_call(
        functools.partial(prep_kernel, tiles, slots),
        out_shape=[shape_of((1, 128), jnp.int32), shape_of((4, 128), jnp.int32)]
        + [slot_shape] * 2
        + out_pieces,
        in_specs=[SMEM] * 4 + [ANY] * 2,
        out_specs=[SMEM] * 2 + [ANY] * 2 + [VMEM] * len(out_pieces),
        scratch_shapes=[
            pltpu.VMEM((slots, size, size), bf16),
            pltpu.VMEM((slots, size, size), bf16),
            pltpu.VMEM((GROUP, 2, size, size), bf16),
            pltpu.SMEM((slots,), jnp.int32),
            pltpu.SMEM((tiles + 2,), jnp.int32),
        ]
        + [pltpu.SemaphoreType.DMA((slots // GROUP,))] * 4,
        compiler_params=params(BIG),
        cost_estimate=pl.CostEstimate(flops=10**9, bytes_accessed=48 * MIB, transcendentals=0),
        name="prep",
    )(row, tile_patient, tile_lab, tile_count, x, w)
    (meta, work, xs, ws), same, other = prep[:4], prep[4:-1], prep[-1]

    early = size - size // 4
    given = lab_factors.reshape(owned_tiles, size, rank)
    late = given[:, early:]
    late = [late] + [swap(late, 2 * h) for h in range(1, rows // 2)]
    own = to_columns(given[:, :early])
    labs = lax.all_gather(own, "rows", axis=0, tiled=True)
    late, _ = lax.optimization_barrier((late, own))
    late_here = to_columns(jnp.stack(late, axis=1))
    late_there = swap(late_here, 1)
    other = swap(other, 1)

    embed_map = ecg_map.astype(f32)
    gram = jnp.dot(embed_map.T, embed_map, precision=highest)
    share_at = lax.axis_index("cols") * share_rows
    start_share = lax.dynamic_slice_in_dim(patient_factors, share_at, share_rows).astype(f32)
    embed_share = lax.dynamic_slice_in_dim(ecg_embed, share_at, share_rows).astype(f32)
    side = (
        jnp.dot(
            embed_share - jnp.dot(start_share, embed_map.T, precision=highest),
            embed_map,
            precision=highest,
        )
        - ridge_term * start_share
    )

    labs, late_here, late_there, same, other = lax.optimization_barrier(
        (labs, late_here, late_there, same, other)
    )
    pieces = [jnp.stack([same[h], other[h]]) for h in range(1, rows // 2)]
    pieces = [swap(piece, 2 * h) for h, piece in enumerate(pieces, 1)]
    own_labs = jnp.concatenate([own, late_here[:, 0]], axis=1)

    def exchange(partial):
        partial = partial.reshape(patient_rows, rank)
        recv = lax.all_to_all(partial, "cols", split_axis=0, concat_axis=0, tiled=True)
        return recv.reshape(cols, share_rows, rank)

    def to_all(probe):
        probe = probe.reshape(patient_rows, rank)
        probe = lax.all_to_all(probe, "cols", split_axis=0, concat_axis=0, tiled=True)
        return probe.reshape(tiles, size, rank)

    state_shape = shape_of((4, share_rows, rank), f32)
    probe_shape = shape_of((cols, share_rows, rank), bf16)
    batches = slots // GROUP
    partial, slot_labs, turned_labs = pl.pallas_call(
        functools.partial(first_pass_kernel, slots, rows),
        out_shape=[
            shape_of((tiles, size, rank), PASS_TYPES[0]),
            shape_of((slots, size, rank), bf16),
            shape_of((slots, rank, size), bf16),
        ],
        in_specs=[SMEM] * 3 + [VMEM] * 3 + [ANY] * 3,
        out_specs=[VMEM, ANY, ANY],
        scratch_shapes=[
            pltpu.VMEM((slots, size, rank), bf16),
            pltpu.VMEM((slots, size, size), bf16),
            pltpu.VMEM((slots, size, size), bf16),
            pltpu.VMEM((tiles, size, rank), f32),
        ]
        + [pltpu.SemaphoreType.DMA((batches,))] * 4
        + [pltpu.VMEM((slots, rank, size), bf16), pltpu.SemaphoreType.DMA((batches,))],
        compiler_params=params(BIG),
        name="first_pass",
    )(
        row,
        meta,
        work,
        xs,
        ws,
        patient_factors.reshape(tiles, size, rank),
        labs,
        late_here,
        late_there,
    )
    state, probe = pl.pallas_call(
        first_kernel,
        out_shape=[state_shape, probe_shape],
        in_specs=[VMEM] * 4,
        out_specs=[VMEM] * 2,
        compiler_params=params(8),
        name="first_step",
    )(exchange(partial), start_share, side, gram)

    def turn(iteration, carry):
        state, probe = carry
        partial = pl.pallas_call(
            functools.partial(pass_kernel, slots),
            out_shape=shape_of((tiles, size, rank), PASS_TYPES[1]),
            in_specs=[SMEM] * 2 + [ANY] * 3 + [VMEM],
            out_specs=VMEM,
            scratch_shapes=[
                pltpu.VMEM((slots, size, size), bf16),
                pltpu.VMEM((slots, size, rank), bf16),
                pltpu.VMEM((slots, rank, size), bf16),
                pltpu.VMEM((tiles, size, rank), f32),
                pltpu.SemaphoreType.DMA((batches,)),
                pltpu.SemaphoreType.DMA((batches,)),
                pltpu.SemaphoreType.DMA((batches,)),
            ],
            compiler_params=params(28),
            name="patient_pass",
        )(meta, work, ws, slot_labs, turned_labs, to_all(probe))
        state, probe = pl.pallas_call(
            step_kernel,
            out_shape=[state_shape, probe_shape],
            in_specs=[SMEM] + [VMEM] * 3,
            out_specs=[VMEM] * 2,
            compiler_params=params(8),
            name="step",
        )(iteration.reshape(1), exchange(partial), state, gram)
        return state, probe

    own_labs, state, probe = lax.optimization_barrier((own_labs, state, probe))
    state, probe = lax.fori_loop(0, ITERS, turn, (state, probe))
    patient_out = state[0]

    f_own = to_all(probe)
    half = tiles // 2
    f_two, f_six = swap(f_own, 2), swap(f_own, 6)
    f_top, f_low = swap(f_six[:half], 2), swap(f_two[half:], 6)
    here = [f_own, f_two, f_six, f_top, f_low]
    factors = here + [swap(part, 1) for part in here]
    delta = pl.pallas_call(
        functools.partial(lab_kernel, slots, rows),
        out_shape=shape_of((col_tiles, lab_share, rank), bf16),
        in_specs=[SMEM] + [ANY] * (2 + len(pieces) + len(factors) + 3),
        out_specs=VMEM,
        scratch_shapes=[
            pltpu.VMEM((rows, 2 * slots + 1, lab_share, size), bf16),
            pltpu.VMEM((rows * tiles, size, rank), bf16),
            pltpu.VMEM((col_tiles, lab_share, rank), bf16),
            pltpu.VMEM((col_tiles, lab_share, rank), f32),
            pltpu.VMEM((col_tiles, lab_share, rank), bf16),
            pltpu.VMEM((col_tiles, lab_share, size), f32),
            pltpu.SemaphoreType.DMA((rows,)),
            pltpu.SemaphoreType.DMA((rows,)),
            pltpu.SemaphoreType.DMA,
            pltpu.VMEM((rows, lab_share, size), bf16),
            pltpu.VMEM((rows, size), jnp.int32),
            pltpu.SMEM((rows, size), jnp.int32),
            pltpu.SemaphoreType.DMA((rows,)),
            pltpu.SemaphoreType.DMA,
        ],
        compiler_params=params(44),
        name="lab_step",
    )(row, same[0], other, *pieces, *factors, labs, late_here, late_there)
    back = lax.all_to_all(
        delta.reshape(col_tiles * lab_share, rank), "rows", split_axis=0, concat_axis=0, tiled=True
    )
    back = back.reshape(rows, owned_tiles, lab_share, rank).transpose(1, 0, 2, 3)
    updated = own_labs.reshape(owned_tiles, rows, lab_share, rank).astype(f32) + back.astype(f32)
    return (patient_out, updated.reshape(1, owned_tiles * size, rank))


def solution(mesh):
    in_specs = (
        P(("rows", "cols"), None),
        P("rows", None),
        P("rows", "cols", None, None),
        P("rows", "cols", None, None),
        P("rows", "cols"),
        P("rows", "cols"),
        P("rows", "cols"),
        P("rows", None),
        P(),
    )
    out_specs = (P(("rows", "cols"), None), P("cols", "rows", None))
    return jax.shard_map(shards, mesh=mesh, in_specs=in_specs, out_specs=out_specs, check_vma=False)
```

```python
import functools

import jax
import jax.numpy as jnp
from jax import lax
from jax.experimental import pallas as pl
from jax.experimental.pallas import tpu as pltpu
from jax.sharding import PartitionSpec as P

ITERS = 3
ridge_term = 1.0
highest = lax.Precision.HIGHEST
bf16 = jnp.bfloat16
f32 = jnp.float32
MIB = 1 << 20
BIG = 56

VMEM = pl.BlockSpec(memory_space=pltpu.VMEM)
SMEM = pl.BlockSpec(memory_space=pltpu.SMEM)
ANY = pl.BlockSpec(memory_space=pl.ANY)

GROUP = 8
CHUNK = 6
LAB_CHUNK = 8
SIDE = 5
PASS_TYPES = (f32, bf16)


def dot_nt(a, b):
    return lax.dot_general(a, b, (((1,), (1,)), ((), ())), preferred_element_type=f32)


def dot_nn(a, b):
    return lax.dot_general(a, b, (((1,), (0,)), ((), ())), preferred_element_type=f32)


def prep_kernel(
    tiles, slots, row_ref, patient_ref, lab_ref, count_ref, x_any, w_any, meta_ref, work_ref, xs_any, ws_any, *rest
):
    x_ref, w_ref, tmp, order, fill, x_sem, w_sem, xs_sem, ws_sem = rest[-9:]
    same, other = rest[:-10], rest[-10]
    n = 2 * len(same)
    pieces = [same[k // 2] if k % 2 == 0 else other.at[k // 2] for k in range(n)]
    share = x_any.shape[2] // n
    live = count_ref[0, 0]
    row = row_ref[0]

    def clear(i, carry):
        meta_ref[0, i] = 0
        return carry

    lax.fori_loop(0, meta_ref.shape[1], clear, 0)
    for p in range(tiles + 2):
        fill[p] = 0

    def key_of(s):
        return jnp.where(s < live, patient_ref[0, s], tiles)

    def count(s, carry):
        key = key_of(s)
        fill[key + 1] = fill[key + 1] + 1
        return carry

    lax.fori_loop(0, slots, count, 0)
    for p in range(tiles + 1):
        fill[p + 1] = fill[p + 1] + fill[p]
        meta_ref[0, slots + p] = fill[p]

    def place(s, carry):
        key = key_of(s)
        at = fill[key]
        fill[key] = at + 1
        order[at] = s
        meta_ref[0, at] = lab_ref[0, s]
        return carry

    lax.fori_loop(0, slots, place, 0)

    def at(c):
        return pl.ds(c * GROUP, GROUP)

    def fetch(c, carry):
        for j in range(GROUP):
            s = c * GROUP + j
            pltpu.make_async_copy(x_any.at[order[s]], x_ref.at[s], x_sem.at[c]).start()
            pltpu.make_async_copy(w_any.at[order[s]], w_ref.at[s], w_sem.at[c]).start()
        return carry

    lax.fori_loop(0, slots // GROUP, fetch, 0)

    def hand_on(c):
        return (
            pltpu.make_async_copy(x_ref.at[at(c)], xs_any.at[at(c)], xs_sem.at[c]),
            pltpu.make_async_copy(w_ref.at[at(c)], ws_any.at[at(c)], ws_sem.at[c]),
        )

    def no_work(i, carry):
        for f in range(4):
            work_ref[f, i] = 0
        return carry

    lax.fori_loop(0, work_ref.shape[1], no_work, 0)
    chunks = jnp.int32(0)
    for p in range(tiles):
        lo, hi = meta_ref[0, slots + p], meta_ref[0, slots + p + 1]

        def add(i, carry, p=p, lo=lo, hi=hi, chunks=chunks):
            work_ref[0, chunks + i] = p
            work_ref[1, chunks + i] = lo + i * CHUNK
            work_ref[2, chunks + i] = hi
            return carry

        count_p = (hi - lo + CHUNK - 1) // CHUNK
        lax.fori_loop(0, count_p, add, 0)
        chunks = chunks + count_p

    def pad(i, carry):
        work_ref[2, i] = live
        work_ref[1, i] = live
        return carry

    blocks = (chunks + SIDE - 1) // SIDE
    lax.fori_loop(chunks, blocks * SIDE, pad, 0)
    work_ref[3, 0] = blocks

    lane = lax.broadcasted_iota(jnp.int32, (share, meta_ref.shape[1]), 1)
    table = jnp.zeros(lane.shape, f32)
    for i in range(slots + tiles + 1):
        table = jnp.where(lane == i, meta_ref[0, i].astype(f32), table)
    for k in range(n):
        pieces[k][2 * slots] = table.astype(bf16)

    size = x_any.shape[1]
    eye = (
        lax.broadcasted_iota(jnp.int32, (size, size), 0)
        == lax.broadcasted_iota(jnp.int32, (size, size), 1)
    ).astype(f32).astype(bf16)

    def turn(c, carry):
        pltpu.make_async_copy(x_any.at[at(c)], x_ref.at[at(c)], x_sem.at[c]).wait()
        pltpu.make_async_copy(w_any.at[at(c)], w_ref.at[at(c)], w_sem.at[c]).wait()
        for copy in hand_on(c):
            copy.start()
        for u in range(GROUP):
            tmp[u, 0] = dot_nt(eye, x_ref[c * GROUP + u]).astype(bf16)
            tmp[u, 1] = dot_nt(eye, w_ref[c * GROUP + u]).astype(bf16)
        for u in range(GROUP):
            s = c * GROUP + u
            for k in range(n):
                rows = pl.ds(pl.multiple_of((row ^ k) * share, share), share)
                pieces[k][s] = tmp[u, 0, rows, :]
                pieces[k][slots + s] = tmp[u, 1, rows, :]
        return carry

    lax.fori_loop(0, slots // GROUP, turn, 0)

    def end(c, carry):
        for copy in hand_on(c):
            copy.wait()
        return carry

    lax.fori_loop(0, slots // GROUP, end, 0)


def patient_sums(with_values, work_ref, x_ref, w_ref, v_ref, t_ref, y_ref, out_ref, acc, arrive):

    def chunk(c):
        tile, first, end = [work_ref[f, c] for f in range(3)]
        at = [jnp.maximum(jnp.minimum(first + j, end - 1), 0) for j in range(CHUNK)]
        labs = jnp.concatenate([v_ref[a] for a in at], axis=0)
        turned = jnp.concatenate([t_ref[a] for a in at], axis=1)
        wts = jnp.concatenate(
            [w_ref[a].astype(f32) * (first + j < end).astype(f32) for j, a in enumerate(at)], axis=1
        )
        scores = dot_nn(y_ref[tile], turned)
        if with_values:
            vals = jnp.concatenate([x_ref[a].astype(f32) for a in at], axis=1)
            kern = wts * (vals - scores)
        else:
            kern = wts * scores
        return tile, dot_nn(kern.astype(bf16), labs)

    def block(b, there):
        there = arrive(there, work_ref[2, b * SIDE + SIDE - 1])
        found = [chunk(b * SIDE + j) for j in range(SIDE)]
        for tile, terms in found:
            acc[tile] += terms
        return there

    lax.fori_loop(0, work_ref[3, 0], block, jnp.int32(1))
    out_ref[...] = acc[...].astype(out_ref.dtype)


def first_pass_kernel(
    slots, n, row_ref, meta_ref, work_ref, xs_any, ws_any, y_ref, early_any, here_any, there_any, *refs
):
    out_ref, kept_any, turned_any, v_ref, w_ref, x_ref, acc, v_sem, w_sem, x_sem, kept_sem = refs[:11]
    t_ref, turned_sem = refs[11:]
    row = row_ref[0]
    live = meta_ref[0, slots + y_ref.shape[0]]
    batches = (live + GROUP - 1) // GROUP
    owned = early_any.shape[0] // n
    early = early_any.shape[1]
    late = v_ref.shape[1] - early

    def at(c):
        return pl.ds(c * GROUP, GROUP)

    def rest(c):
        return (
            pltpu.make_async_copy(ws_any.at[at(c)], w_ref.at[at(c)], w_sem.at[c]),
            pltpu.make_async_copy(xs_any.at[at(c)], x_ref.at[at(c)], x_sem.at[c]),
        )

    def keep(c):
        return (
            pltpu.make_async_copy(v_ref.at[at(c)], kept_any.at[at(c)], kept_sem.at[c]),
            pltpu.make_async_copy(t_ref.at[at(c)], turned_any.at[at(c)], turned_sem.at[c]),
        )

    def start(c, carry):
        for j in range(GROUP):
            s = c * GROUP + j
            tile = meta_ref[0, s]
            source = row ^ (tile // owned)
            pltpu.make_async_copy(
                early_any.at[tile], v_ref.at[s, pl.ds(0, early), :], v_sem.at[c]
            ).start()
            for core, late_any in enumerate((here_any, there_any)):

                @pl.when(source % 2 == core)
                def _(late_any=late_any, s=s, tile=tile, source=source):
                    pltpu.make_async_copy(
                        late_any.at[tile % owned, source // 2],
                        v_ref.at[s, pl.ds(early, late), :],
                        v_sem.at[c],
                    ).start()

        for copy in rest(c):
            copy.start()
        return carry

    lax.fori_loop(0, batches, start, 0)

    def wait(c, carry):
        for copy in rest(c):
            copy.wait()
        pltpu.make_async_copy(kept_any.at[at(c)], v_ref.at[at(c)], v_sem.at[c]).wait()
        for j in range(GROUP):
            t_ref[c * GROUP + j] = v_ref[c * GROUP + j].T
        for copy in keep(c):
            copy.start()
        return carry

    acc[...] = jnp.zeros_like(acc)
    wait(0, 0)

    def arrive(there, hi):
        until = jnp.maximum((hi + GROUP - 1) // GROUP, there)
        lax.fori_loop(there, until, wait, 0)
        return until

    patient_sums(True, work_ref, x_ref, w_ref, v_ref, t_ref, y_ref, out_ref, acc, arrive)

    def end(c, carry):
        for copy in keep(c):
            copy.wait()
        return carry

    lax.fori_loop(0, batches, end, 0)


def pass_kernel(slots, meta_ref, work_ref, ws_any, kept_any, turned_any, y_ref, out_ref, *refs):
    w_ref, v_ref, t_ref, acc, w_sem, v_sem, t_sem = refs
    batches = (meta_ref[0, slots + y_ref.shape[0]] + GROUP - 1) // GROUP

    def copies(c):
        at = pl.ds(c * GROUP, GROUP)
        return (
            pltpu.make_async_copy(ws_any.at[at], w_ref.at[at], w_sem.at[c]),
            pltpu.make_async_copy(turned_any.at[at], t_ref.at[at], t_sem.at[c]),
            pltpu.make_async_copy(kept_any.at[at], v_ref.at[at], v_sem.at[c]),
        )

    def start(c, carry):
        for copy in copies(c):
            copy.start()
        return carry

    def wait(c, carry):
        for copy in copies(c):
            copy.wait()
        return carry

    lax.fori_loop(0, batches, start, 0)
    acc[...] = jnp.zeros_like(acc)
    wait(0, 0)

    def arrive(there, hi):
        until = jnp.maximum((hi + GROUP - 1) // GROUP, there)
        lax.fori_loop(there, until, wait, 0)
        return until

    patient_sums(False, work_ref, None, w_ref, v_ref, t_ref, y_ref, out_ref, acc, arrive)


def spread(probe_ref, rows):
    for k in range(probe_ref.shape[0]):
        probe_ref[k] = rows


def first_kernel(recv_ref, start_ref, side_ref, gram_ref, state_ref, probe_ref):
    residual = jnp.sum(recv_ref[...].astype(f32), axis=0) + side_ref[...]
    state_ref[0] = start_ref[...].astype(f32)
    state_ref[1] = residual
    state_ref[2] = residual
    state_ref[3] = (
        jnp.dot(residual, gram_ref[...], precision=highest, preferred_element_type=f32)
        + ridge_term * residual
    )
    spread(probe_ref, residual.astype(bf16))


def step_kernel(turn_ref, recv_ref, state_in, gram_ref, state_ref, probe_ref):
    residual = state_in[1]
    direction = state_in[2]
    applied = jnp.sum(recv_ref[...].astype(f32), axis=0) + state_in[3]
    norm_now = jnp.sum(residual * residual, axis=1, keepdims=True)
    step_size = norm_now / jnp.sum(direction * applied, axis=1, keepdims=True)
    solution_now = state_in[0] + step_size * direction
    state_ref[0] = solution_now
    last = turn_ref[0] == ITERS - 1

    @pl.when(last)
    def _():
        spread(probe_ref, solution_now.astype(bf16))

    @pl.when(jnp.logical_not(last))
    def _():
        residual_next = residual - step_size * applied
        norm_next = jnp.sum(residual_next * residual_next, axis=1, keepdims=True)
        direction_next = residual_next + norm_next / norm_now * direction
        state_ref[1] = residual_next
        state_ref[2] = direction_next
        state_ref[3] = (
            jnp.dot(
                direction_next, gram_ref[...], precision=highest, preferred_element_type=f32
            )
            + ridge_term * direction_next
        )
        spread(probe_ref, direction_next.astype(bf16))


def lab_kernel(slots, n, row_ref, same_any, other_any, *refs):
    pieces = [same_any, other_any.at[0]]
    for ref in refs[: n // 2 - 1]:
        pieces += [ref.at[0], ref.at[1]]
    refs = refs[n // 2 - 1 :]
    f_own, f_two, f_six, f_top, f_low, g_own, g_two, g_six, g_top, g_low = refs[:10]
    early_any, here_any, there_any, out_ref, xw, f_ref, v_ref, acc, probe, curv, p_sem, f_sem, v_sem = refs[10:23]
    coded, table, meta_ref, t_sem, m_sem = refs[23:]
    tiles = f_ref.shape[0] // n
    half = tiles // 2
    share = v_ref.shape[1]
    size = f_ref.shape[1]
    row = row_ref[0]
    t_copies = [
        pltpu.make_async_copy(pieces[k].at[2 * slots], coded.at[k], t_sem.at[k]) for k in range(n)
    ]
    for copy in t_copies:
        copy.start()
    early = early_any.shape[1] // share
    owned = v_ref.shape[0] // n

    @pl.when(row < early)
    def _():
        at = pl.ds(row * share, share)
        pltpu.make_async_copy(early_any.at[:, at, :], v_ref, v_sem).start()

    @pl.when(row >= early)
    def _():
        at = pl.ds((row - early) * share, share)
        for k in range(n):
            part = (here_any, there_any)[k % 2].at[:, k // 2, at, :]
            to = pl.ds((row ^ k) * owned, owned)
            pltpu.make_async_copy(part, v_ref.at[to], v_sem).start()

    factors = {0: [f_own], 1: [g_own], 2: [f_two], 3: [g_two], 6: [f_six], 7: [g_six]}
    factors |= {4: [f_top, f_low], 5: [g_top, g_low]}
    for k in range(n):
        pltpu.make_async_copy(pieces[k], xw.at[k], p_sem.at[k]).start()
        for h, ref in enumerate(factors[k]):
            to = pl.ds((row ^ k) * tiles + h * half, ref.shape[0])
            pltpu.make_async_copy(ref, f_ref.at[to], f_sem.at[k]).start()
    acc[...] = jnp.zeros_like(acc)
    for k, copy in enumerate(t_copies):
        copy.wait()
        table[k : k + 1] = coded[k].astype(f32).astype(jnp.int32)[0:1]
    m_copy = pltpu.make_async_copy(table, meta_ref, m_sem)
    m_copy.start()
    curv[...] = jnp.zeros_like(curv)
    m_copy.wait()
    pltpu.make_async_copy(v_ref, v_ref, v_sem).wait()

    span = LAB_CHUNK * share
    row_slot = lax.broadcasted_iota(jnp.int32, (span, size), 0) // share

    def sweep(terms_of, total, arrive):
        def of_source(k, carry):
            source = row ^ k
            arrive(k, source)
            lo = [meta_ref[k, slots + p] for p in range(tiles)]
            hi = [meta_ref[k, slots + p + 1] for p in range(tiles)]

            def block(i, carry):
                found = []
                for p in range(tiles):
                    first = lo[p] + i * LAB_CHUNK
                    base = jnp.minimum(first, slots - LAB_CHUNK)
                    labs = [meta_ref[k, base + j] for j in range(LAB_CHUNK)]
                    inside = (row_slot >= first - base) & (row_slot < hi[p] - base)
                    wts = xw[k, pl.ds(slots + base, LAB_CHUNK)].reshape(span, size).astype(f32)
                    wts = jnp.where(inside, wts, 0.0)
                    found.append((labs, terms_of(k, base, labs, wts, f_ref[source * tiles + p])))
                for labs, terms in found:
                    for j, t in enumerate(labs):
                        total[t] += terms[j * share : (j + 1) * share]
                return carry

            most = functools.reduce(jnp.maximum, [b - a for a, b in zip(lo, hi)])
            return lax.fori_loop(0, (most + LAB_CHUNK - 1) // LAB_CHUNK, block, carry)

        lax.fori_loop(0, n, of_source, 0)

    def residual_terms(k, base, labs, wts, patients):
        rows = jnp.concatenate([v_ref[t] for t in labs], axis=0)
        vals = xw[k, pl.ds(base, LAB_CHUNK)].reshape(span, size).astype(f32)
        return dot_nn((wts * (vals - dot_nt(rows, patients))).astype(bf16), patients)

    def arrive(k, source):
        pltpu.make_async_copy(xw.at[0], xw.at[k], p_sem.at[k]).wait()
        at = pl.ds(source * tiles, tiles)
        pltpu.make_async_copy(f_ref.at[pl.ds(0, tiles)], f_ref.at[at], f_sem.at[k]).wait()

    sweep(residual_terms, acc, arrive)

    block = 16

    def finish(i, carry):
        at = pl.ds(i * block, block)
        rest = acc[at] - ridge_term * v_ref[at].astype(f32)
        acc[at] = rest
        probe[at] = rest.astype(bf16)
        return carry

    lax.fori_loop(0, acc.shape[0] // block, finish, 0)

    def curvature_terms(k, base, labs, wts, patients):
        rows = jnp.concatenate([probe[t] for t in labs], axis=0)
        inner = dot_nt(rows, patients)
        return wts * inner * inner

    sweep(curvature_terms, curv, lambda k, source: None)

    def emit(i, carry):
        at = pl.ds(i * block, block)
        rest = acc[at]
        norm = jnp.sum(rest * rest, axis=-1, keepdims=True)
        total = jnp.sum(curv[at], axis=-1, keepdims=True) + ridge_term * norm
        out_ref[at] = (norm / total * rest).astype(out_ref.dtype)
        return carry

    lax.fori_loop(0, acc.shape[0] // block, emit, 0)


def shape_of(shape, dtype):
    return jax.ShapeDtypeStruct(shape, dtype)


def params(mib):
    return pltpu.CompilerParams(vmem_limit_bytes=mib * MIB)


def shards(
    lab_factors,
    patient_factors,
    values,
    weights,
    tile_patient,
    tile_lab,
    tile_count,
    ecg_embed,
    ecg_map,
):
    rows = lax.axis_size("rows")
    cols = lax.axis_size("cols")
    size = values.shape[2]
    slots = values.shape[1]
    rank = lab_factors.shape[1]
    owned_tiles = lab_factors.shape[0] // size
    col_tiles = owned_tiles * rows
    patient_rows = patient_factors.shape[0]
    tiles = patient_rows // size
    share_rows = patient_rows // cols
    lab_share = size // rows
    row = lax.axis_index("rows").astype(jnp.int32).reshape(1)
    x, w = values[0], weights[0]

    def swap(array, k):
        return lax.ppermute(array, "rows", [(i, i ^ k) for i in range(rows)])

    def to_columns(array):
        return lax.all_to_all(array, "cols", split_axis=0, concat_axis=0, tiled=True)

    slot_shape = shape_of((slots, size, size), bf16)
    piece = (2 * slots + 1, lab_share, size)
    out_pieces = [shape_of(piece, bf16)] * (rows // 2) + [shape_of((rows // 2, *piece), bf16)]
    prep = pl.pallas_call(
        functools.partial(prep_kernel, tiles, slots),
        out_shape=[shape_of((1, 128), jnp.int32), shape_of((4, 128), jnp.int32)]
        + [slot_shape] * 2
        + out_pieces,
        in_specs=[SMEM] * 4 + [ANY] * 2,
        out_specs=[SMEM] * 2 + [ANY] * 2 + [VMEM] * len(out_pieces),
        scratch_shapes=[
            pltpu.VMEM((slots, size, size), bf16),
            pltpu.VMEM((slots, size, size), bf16),
            pltpu.VMEM((GROUP, 2, size, size), bf16),
            pltpu.SMEM((slots,), jnp.int32),
            pltpu.SMEM((tiles + 2,), jnp.int32),
        ]
        + [pltpu.SemaphoreType.DMA((slots // GROUP,))] * 4,
        compiler_params=params(BIG),
        cost_estimate=pl.CostEstimate(flops=10**9, bytes_accessed=48 * MIB, transcendentals=0),
        name="prep",
    )(row, tile_patient, tile_lab, tile_count, x, w)
    (meta, work, xs, ws), same, other = prep[:4], prep[4:-1], prep[-1]

    early = size - size // 4
    given = lab_factors.reshape(owned_tiles, size, rank)
    late = given[:, early:]
    late = [late] + [swap(late, 2 * h) for h in range(1, rows // 2)]
    own = to_columns(given[:, :early])
    labs = lax.all_gather(own, "rows", axis=0, tiled=True)
    late, _ = lax.optimization_barrier((late, own))
    late_here = to_columns(jnp.stack(late, axis=1))
    late_there = swap(late_here, 1)
    other = swap(other, 1)

    embed_map = ecg_map.astype(f32)
    gram = jnp.dot(embed_map.T, embed_map, precision=highest)
    share_at = lax.axis_index("cols") * share_rows
    start_share = lax.dynamic_slice_in_dim(patient_factors, share_at, share_rows).astype(f32)
    embed_share = lax.dynamic_slice_in_dim(ecg_embed, share_at, share_rows).astype(f32)
    side = (
        jnp.dot(
            embed_share - jnp.dot(start_share, embed_map.T, precision=highest),
            embed_map,
            precision=highest,
        )
        - ridge_term * start_share
    )

    labs, late_here, late_there, same, other = lax.optimization_barrier(
        (labs, late_here, late_there, same, other)
    )
    pieces = [jnp.stack([same[h], other[h]]) for h in range(1, rows // 2)]
    pieces = [swap(piece, 2 * h) for h, piece in enumerate(pieces, 1)]
    own_labs = jnp.concatenate([own, late_here[:, 0]], axis=1)

    def exchange(partial):
        partial = partial.reshape(patient_rows, rank)
        recv = lax.all_to_all(partial, "cols", split_axis=0, concat_axis=0, tiled=True)
        return recv.reshape(cols, share_rows, rank)

    def to_all(probe):
        probe = probe.reshape(patient_rows, rank)
        probe = lax.all_to_all(probe, "cols", split_axis=0, concat_axis=0, tiled=True)
        return probe.reshape(tiles, size, rank)

    state_shape = shape_of((4, share_rows, rank), f32)
    probe_shape = shape_of((cols, share_rows, rank), bf16)
    batches = slots // GROUP
    partial, slot_labs, turned_labs = pl.pallas_call(
        functools.partial(first_pass_kernel, slots, rows),
        out_shape=[
            shape_of((tiles, size, rank), PASS_TYPES[0]),
            shape_of((slots, size, rank), bf16),
            shape_of((slots, rank, size), bf16),
        ],
        in_specs=[SMEM] * 3 + [VMEM] * 3 + [ANY] * 3,
        out_specs=[VMEM, ANY, ANY],
        scratch_shapes=[
            pltpu.VMEM((slots, size, rank), bf16),
            pltpu.VMEM((slots, size, size), bf16),
            pltpu.VMEM((slots, size, size), bf16),
            pltpu.VMEM((tiles, size, rank), f32),
        ]
        + [pltpu.SemaphoreType.DMA((batches,))] * 4
        + [pltpu.VMEM((slots, rank, size), bf16), pltpu.SemaphoreType.DMA((batches,))],
        compiler_params=params(BIG),
        name="first_pass",
    )(
        row,
        meta,
        work,
        xs,
        ws,
        patient_factors.reshape(tiles, size, rank),
        labs,
        late_here,
        late_there,
    )
    state, probe = pl.pallas_call(
        first_kernel,
        out_shape=[state_shape, probe_shape],
        in_specs=[VMEM] * 4,
        out_specs=[VMEM] * 2,
        compiler_params=params(8),
        name="first_step",
    )(exchange(partial), start_share, side, gram)

    def turn(iteration, carry):
        state, probe = carry
        partial = pl.pallas_call(
            functools.partial(pass_kernel, slots),
            out_shape=shape_of((tiles, size, rank), PASS_TYPES[1]),
            in_specs=[SMEM] * 2 + [ANY] * 3 + [VMEM],
            out_specs=VMEM,
            scratch_shapes=[
                pltpu.VMEM((slots, size, size), bf16),
                pltpu.VMEM((slots, size, rank), bf16),
                pltpu.VMEM((slots, rank, size), bf16),
                pltpu.VMEM((tiles, size, rank), f32),
                pltpu.SemaphoreType.DMA((batches,)),
                pltpu.SemaphoreType.DMA((batches,)),
                pltpu.SemaphoreType.DMA((batches,)),
            ],
            compiler_params=params(28),
            name="patient_pass",
        )(meta, work, ws, slot_labs, turned_labs, to_all(probe))
        state, probe = pl.pallas_call(
            step_kernel,
            out_shape=[state_shape, probe_shape],
            in_specs=[SMEM] + [VMEM] * 3,
            out_specs=[VMEM] * 2,
            compiler_params=params(8),
            name="step",
        )(iteration.reshape(1), exchange(partial), state, gram)
        return state, probe

    own_labs, state, probe = lax.optimization_barrier((own_labs, state, probe))
    state, probe = lax.fori_loop(0, ITERS, turn, (state, probe))
    patient_out = state[0]

    f_own = to_all(probe)
    half = tiles // 2
    f_two, f_six = swap(f_own, 2), swap(f_own, 6)
    f_top, f_low = swap(f_six[:half], 2), swap(f_two[half:], 6)
    here = [f_own, f_two, f_six, f_top, f_low]
    factors = here + [swap(part, 1) for part in here]
    delta = pl.pallas_call(
        functools.partial(lab_kernel, slots, rows),
        out_shape=shape_of((col_tiles, lab_share, rank), bf16),
        in_specs=[SMEM] + [ANY] * (2 + len(pieces) + len(factors) + 3),
        out_specs=VMEM,
        scratch_shapes=[
            pltpu.VMEM((rows, 2 * slots + 1, lab_share, size), bf16),
            pltpu.VMEM((rows * tiles, size, rank), bf16),
            pltpu.VMEM((col_tiles, lab_share, rank), bf16),
            pltpu.VMEM((col_tiles, lab_share, rank), f32),
            pltpu.VMEM((col_tiles, lab_share, rank), bf16),
            pltpu.VMEM((col_tiles, lab_share, size), f32),
            pltpu.SemaphoreType.DMA((rows,)),
            pltpu.SemaphoreType.DMA((rows,)),
            pltpu.SemaphoreType.DMA,
            pltpu.VMEM((rows, lab_share, size), bf16),
            pltpu.VMEM((rows, size), jnp.int32),
            pltpu.SMEM((rows, size), jnp.int32),
            pltpu.SemaphoreType.DMA((rows,)),
            pltpu.SemaphoreType.DMA,
        ],
        compiler_params=params(36),
        name="lab_step",
    )(row, same[0], other, *pieces, *factors, labs, late_here, late_there)
    back = lax.all_to_all(
        delta.reshape(col_tiles * lab_share, rank), "rows", split_axis=0, concat_axis=0, tiled=True
    )
    back = back.reshape(rows, owned_tiles, lab_share, rank).transpose(1, 0, 2, 3)
    updated = own_labs.reshape(owned_tiles, rows, lab_share, rank).astype(f32) + back.astype(f32)
    return (patient_out, updated.reshape(1, owned_tiles * size, rank))


def solution(mesh):
    in_specs = (
        P(("rows", "cols"), None),
        P("rows", None),
        P("rows", "cols", None, None),
        P("rows", "cols", None, None),
        P("rows", "cols"),
        P("rows", "cols"),
        P("rows", "cols"),
        P("rows", None),
        P(),
    )
    out_specs = (P(("rows", "cols"), None), P("cols", "rows", None))
    return jax.shard_map(shards, mesh=mesh, in_specs=in_specs, out_specs=out_specs, check_vma=False)
```
